32 devices in a mesh: region: 16 (over z, y, x), split: 2 (over core).
Axes of the slice: x: 2, y: 2, z: 4, core: 2. Of those that a mesh axis runs over, the one named last changes fastest.
Arguments:
- features: bfloat16 [96, 16384], P(None, ('region', 'split')), may hold values from -6 to 6
- kernel_one: bfloat16 [27, 96, 96], replicated, may hold values from -0.125 to 0.125
- kernel_two: bfloat16 [27, 96, 192], replicated, may hold values from -0.125 to 0.125
- occupancy: int32 [32, 512], P(('region', 'split')), may hold values 0 or 1
- neighbors: int32 [32, 27], P(('region', 'split')), may hold values from -1 to 31, as said below
- cotangent: bfloat16 [192, 16384], P(None, ('region', 'split')), may hold values from -0.046875 to 0.046875
Outputs:
- output: bfloat16 [192, 16384], P(None, ('region', 'split'))
- grad_one: float32 [27, 96, 96], replicated
- grad_two: float32 [27, 96, 192], replicated
The draws below stay inside these ranges and needn't reach their ends.
Inputs may be any that keep to these rules, and one draw needn't show every extreme that they name: `neighbors`: entry k = 9 (dx + 1) + 3 (dy + 1) + (dz + 1) of a block's row is the active block whose block coordinates differ by (dx, dy, dz), or -1 if there is none; entry 13 is the block itself. Blocks are numbered in device order. The blocks of region r have x coordinate r and y coordinate 0 or 1; the device of split index s holds the blocks with z coordinate s. So a neighbour in region r - 1 or r + 1 differs by dx = -1 or +1, and a neighbour on the other device of the same region lies across the z boundary between the two halves.
All inputs are finite; a program needn't handle non-finite values. No bound on the sum of `occupancy` on one device may be relied on, other than what follows from the above.
Results may differ from the reference program's by a relative error of at most 0.0049.
Values may be sent and summed in bfloat16 or wider, within the bound.
No kernel may reach another device: no remote copies, remote signals or barrier semaphores. Data moves between devices by JAX's collectives and lax.ppermute only.
A program may use at most 64 MiB of HBM per device.

```python
import jax
import jax.numpy as jnp
import numpy as np
from jax import lax

C1 = 96
C2 = 192
B_DEV = 1
BLOCKS = 32


def draw_neighbors(key, part):
    device_count = BLOCKS // B_DEV
    regions = device_count // 2
    cell_count = 2 * B_DEV
    scores = jax.random.randint(key, (device_count, cell_count), 0, 1 << 20) * cell_count + jnp.arange(cell_count)[None, :]
    picked = jnp.sort(jnp.argsort(scores, axis=1)[:, :B_DEV], axis=1).astype(jnp.int32)
    device_ids = jnp.arange(device_count, dtype=jnp.int32)[:, None]
    coord_x = jnp.broadcast_to(device_ids // 2, (device_count, B_DEV)).reshape(-1)
    coord_y = (picked // B_DEV).reshape(-1)
    coord_z = (device_ids % 2 * B_DEV + picked % B_DEV).reshape(-1)
    block_ids = jnp.arange(BLOCKS, dtype=jnp.int32)
    cell_grid = jnp.full((regions, 2, 2 * B_DEV), -1, jnp.int32).at[coord_x, coord_y, coord_z].set(block_ids)
    offsets = jnp.arange(27, dtype=jnp.int32)
    target_x = coord_x[:, None] + offsets[None, :] // 9 - 1
    target_y = coord_y[:, None] + offsets[None, :] // 3 % 3 - 1
    target_z = coord_z[:, None] + offsets[None, :] % 3 - 1
    inside = (target_x >= 0) & (target_x < regions) & (target_y >= 0) & (target_y < 2) & (target_z >= 0) & (target_z < 2 * B_DEV)
    located = cell_grid[jnp.clip(target_x, 0, regions - 1), jnp.clip(target_y, 0, 1), jnp.clip(target_z, 0, 2 * B_DEV - 1)]
    return jnp.where(inside, located, -1).astype(jnp.int32)


def touch_ends(entries, own_key, smallest, high):
    extent = entries.shape
    spot = [jax.random.randint(jax.random.fold_in(own_key, axis), (), 0, extent[axis]) for axis in range(len(extent))]
    entries = entries.at[tuple(spot)].set(smallest)
    longest = extent.index(max(extent))
    spot[longest] = (spot[longest] + 1) % extent[longest]
    return entries.at[tuple(spot)].set(high)


def level_of(own_key, extent, split, least, high):
    factor_of = 1.0
    for dim, blocks in split:
        draws = jax.random.uniform(jax.random.fold_in(jax.random.fold_in(own_key, 6), dim), (blocks,), jnp.float32, least / len(split), high / len(split))
        factor_of = factor_of * jnp.repeat(jnp.exp(draws), extent[dim] // blocks).reshape((-1,) + (1,) * (len(extent) - 1 - dim))
    return factor_of


def centred(stream_key, dims, spread, reach, shards=(), held_as=jnp.bfloat16):
    factor_of = level_of(stream_key, dims, shards, -0.22, 0.18) if shards else 1.0
    values = jax.random.normal(stream_key, dims, jnp.float32) * spread * factor_of
    return jnp.minimum(jnp.maximum(values, -reach), reach).astype(held_as)


def setup_inputs(seed: int = 0) -> dict:
    splits = jax.random.split(jax.random.key(seed), 7)
    return {
        "features": centred(splits[0], (C1, BLOCKS * 512), 1.0, 6.0, ((1, 32),)),
        "kernel_one": centred(splits[1], (27, C1, C1), (27 * C1) ** -0.5, 0.125),
        "kernel_two": centred(splits[2], (27, C1, C2), (27 * C1) ** -0.5, 0.125),
        "occupancy": touch_ends((jax.random.randint(splits[3], (BLOCKS, 512), 0, 5) < 3).astype(jnp.int32), jax.random.fold_in(splits[3], 1), 0, 1),
        "neighbors": draw_neighbors(jax.random.fold_in(splits[6], 71), 0),
        "cotangent": centred(splits[5], (C2, BLOCKS * 512), ((BLOCKS * 512) ** -0.5), 0.046875, ((1, 32),)),
    }


def voxel_tables():
    voxels = np.arange(512)
    along_x = voxels // 64
    along_y = (voxels // 8) % 8
    along_z = voxels % 8
    block_code = np.zeros((27, 512), np.int32)
    voxel_code = np.zeros((27, 512), np.int32)
    for offset in range(27):
        moved_x = along_x + offset // 9 - 1
        moved_y = along_y + (offset // 3) % 3 - 1
        moved_z = along_z + offset % 3 - 1
        block_code[offset] = (moved_x // 8 + 1) * 9 + (moved_y // 8 + 1) * 3 + (moved_z // 8 + 1)
        voxel_code[offset] = (moved_x % 8) * 64 + (moved_y % 8) * 8 + moved_z % 8
    return block_code, voxel_code


def convolve(window, lookup, kernel):
    def accumulate(offset, total):
        picked = jnp.take(window, lax.dynamic_index_in_dim(lookup, offset, 0, keepdims=False), axis=1).astype(jnp.float32)
        weights = lax.dynamic_index_in_dim(kernel, offset, 0, keepdims=False).astype(jnp.float32)
        return total + jnp.dot(weights.T, picked, precision=lax.Precision.HIGHEST)
    return lax.fori_loop(0, 27, accumulate, jnp.zeros((kernel.shape[2], lookup.shape[1]), jnp.float32))


def kernel_gradient(window, lookup, gradient):
    gradient_wide = gradient.astype(jnp.float32)

    def accumulate(offset, total):
        picked = jnp.take(window, lax.dynamic_index_in_dim(lookup, offset, 0, keepdims=False), axis=1).astype(jnp.float32)
        product = jnp.dot(picked, gradient_wide.T, precision=lax.Precision.HIGHEST)
        return lax.dynamic_update_index_in_dim(total, product, offset, 0)
    return lax.fori_loop(0, 27, accumulate, jnp.zeros((27, window.shape[0], gradient.shape[0]), jnp.float32))


def convolve_back(window, lookup, kernel):
    def accumulate(offset, total):
        picked = jnp.take(window, lax.dynamic_index_in_dim(lookup, 26 - offset, 0, keepdims=False), axis=1).astype(jnp.float32)
        weights = lax.dynamic_index_in_dim(kernel, offset, 0, keepdims=False).astype(jnp.float32)
        return total + jnp.dot(weights, picked, precision=lax.Precision.HIGHEST)
    return lax.fori_loop(0, 27, accumulate, jnp.zeros((kernel.shape[1], lookup.shape[1]), jnp.float32))


def padded(values):
    return jnp.concatenate([values, jnp.zeros((values.shape[0], 1), values.dtype)], axis=1)


def reference(features, kernel_one, kernel_two, occupancy, neighbors, cotangent):
    tables = voxel_tables()
    columns = features.shape[1]
    block_ids = jnp.transpose(jnp.take(neighbors, jnp.asarray(tables[0]), axis=1), (1, 0, 2))
    voxel_target = jnp.asarray(tables[1])[:, None, :]
    lookup = jnp.where(block_ids < 0, columns, block_ids * 512 + voxel_target).reshape(27, -1).astype(jnp.int32)
    active = (occupancy.reshape(-1) > 0)[None, :]
    zero_value = jnp.zeros((), features.dtype)
    masked = jnp.where(active, features, zero_value)
    hidden_pre = jnp.where(active, convolve(padded(masked), lookup, kernel_one), 0.0)
    hidden = jnp.where(active, jax.nn.silu(hidden_pre), 0.0).astype(jnp.bfloat16)
    output = jnp.where(active, convolve(padded(hidden), lookup, kernel_two), 0.0)
    grad_out = jnp.where(active, cotangent, zero_value)
    grad_two = kernel_gradient(padded(hidden), lookup, grad_out)
    back = convolve_back(padded(grad_out), lookup, kernel_two)
    sigmoid_pre = jax.nn.sigmoid(hidden_pre)
    grad_pre = jnp.where(active, back * sigmoid_pre * (1.0 + hidden_pre * (1.0 - sigmoid_pre)), 0.0).astype(jnp.bfloat16)
    grad_one = kernel_gradient(padded(masked), lookup, grad_pre)
    return (output.astype(jnp.bfloat16), grad_one, grad_two)
```

```python
import functools

import jax
import jax.numpy as jnp
from jax import lax
from jax.experimental import pallas as pl
from jax.experimental.pallas import tpu as pltpu
from jax.sharding import PartitionSpec as P

F32 = jnp.float32
BF16 = jnp.bfloat16
LANES = 128
VMEM_BYTES = 56 * 2**20


def up_to(value, step):
    return -(-value // step) * step


def whole(count):
    return [pl.BlockSpec(memory_space=pltpu.VMEM)] * count


def pack_kernel(features_ref, occupancy_ref, cotangent_ref, packed_ref):
    channels, voxels = features_ref.shape
    outs = cotangent_ref.shape[0]
    active = occupancy_ref[...] > 0
    masked = jnp.where(active, features_ref[...].astype(F32), 0.0)
    flag = jnp.where(active, 1.0, 0.0)
    row = lax.broadcasted_iota(jnp.int32, (LANES - channels, voxels), 0)
    tail = jnp.where(row == 0, jnp.broadcast_to(flag, row.shape), 0.0)
    packed_ref[:, :LANES] = jnp.concatenate([masked, tail], 0).T.astype(BF16)
    grad_out = jnp.where(active, cotangent_ref[...].astype(F32), 0.0)
    spare = up_to(outs, LANES) - outs
    grad_out = jnp.concatenate([grad_out, jnp.zeros((spare, voxels), F32)], 0)
    packed_ref[:, LANES:] = grad_out.T.astype(BF16)


def planes_kernel(position_ref, own_ref, partner_ref, first_ref, second_ref):
    odd = position_ref[0]
    for which, target in enumerate((first_ref, second_ref)):
        upper = 1 - odd if which == 0 else odd
        for source, block in enumerate((own_ref, partner_ref)):
            row = pl.multiple_of(upper * 384, 128)
            near = pl.multiple_of(upper * 448, 64)
            target[source, :, :LANES] = block[pl.ds(row, 128), :LANES]
            target[source, :64, LANES:] = block[pl.ds(near, 64), LANES : 2 * LANES]
            target[source, 64:, LANES:] = block[pl.ds(near, 64), 2 * LANES :]


def weights_kernel(one_ref, two_ref, one_pad_ref, two_pad_ref, two_turned_ref):
    offsets, channels, outs = two_ref.shape
    one_pad_ref[:, :channels, :] = one_ref[...]
    two_pad_ref[:, :channels, :] = two_ref[...]
    spare = LANES - channels
    one_pad_ref[:, channels:, :] = jnp.zeros((offsets, spare, one_ref.shape[2]), BF16)
    two_pad_ref[:, channels:, :] = jnp.zeros((offsets, spare, outs), BF16)
    two_turned_ref[:, outs:, :] = jnp.zeros((offsets, two_turned_ref.shape[1] - outs, channels), BF16)
    for offset in range(offsets):
        two_turned_ref[offset, :outs, :] = two_ref[offset].astype(F32).T.astype(BF16)


def tile_of(offset, offsets):
    group, place = divmod(offset, 4)
    return group, place


def store_gradient(total_ref, product, offset, first_row, rows, channels):
    group, place = tile_of(offset, 27)
    if place < 3:
        base = (3 * group + place) * rows + first_row
        total_ref[base : base + product.shape[0], :channels] = product[:, :channels]
    else:
        spare = LANES - channels
        for piece in range(3):
            base = (3 * group + piece) * rows + first_row
            total_ref[base : base + product.shape[0], channels:] = product[:, piece * spare : (piece + 1) * spare]


def main_kernel(
    position_ref, neighbors_ref, own_ref, partner_ref, first_ref, second_ref, cotangent_ref, occupancy_ref,
    one_ref, two_ref, turned_ref, output_ref, kept_ref, sent_ref, masked_w, grad_w, hidden_w, total,
):
    odd, split = position_ref[0], position_ref[1]
    channels = one_ref.shape[2]
    outs = two_ref.shape[2]
    wide = grad_w.shape[3]
    masked_w[:, 6:18] = jnp.zeros((12, 12, 24, LANES), F32)
    grad_w[:, 7:17] = jnp.zeros((10, 10, 24, wide), F32)

    own = own_ref[...].astype(F32).reshape(8, 8, 8, LANES + wide)
    masked_w[2:10, 8:16, 8:16, :] = own[..., :LANES]
    grad_w[1:9, 8:16, 8:16, :] = own[..., LANES:]

    def placed(step_x, step_z):
        found = [neighbors_ref[0, 9 * (step_x + 1) + 3 * step_y + step_z + 1] >= 0 for step_y in range(3)]
        y = jnp.where(found[0], 0, jnp.where(found[1], 1, 2))
        return found[0] | found[1] | found[2], pl.multiple_of(8 * y, 8)

    step_z = 1 - 2 * split
    valid, y = placed(0, step_z)
    z = pl.multiple_of(8 + 8 * step_z, 8)

    @pl.when(valid)
    def _():
        block = partner_ref[...].astype(F32).reshape(8, 8, 8, LANES + wide)
        masked_w[2:10, pl.ds(y, 8), pl.ds(z, 8), :] = block[..., :LANES]
        grad_w[1:9, pl.ds(y, 8), pl.ds(z, 8), :] = block[..., LANES:]

    for which, ref in enumerate((first_ref, second_ref)):
        step_x = 1 - 2 * odd if which == 0 else 2 * odd - 1
        for source in range(2):
            step_z = 0 if source == 0 else 1 - 2 * split
            valid, y = placed(step_x, step_z)
            z = pl.multiple_of(8 + 8 * step_z, 8)
            x_masked = jnp.where(step_x > 0, 10, 0)
            x_grad = jnp.where(step_x > 0, 9, 0)

            @pl.when(valid)
            def _():
                block = ref[source].astype(F32)
                masked_w[pl.ds(x_masked, 2), pl.ds(y, 8), pl.ds(z, 8), :] = block[:, :LANES].reshape(2, 8, 8, LANES)
                near = jnp.concatenate([block[:64, LANES:], block[64:, LANES:]], 1)
                grad_w[pl.ds(x_grad, 1), pl.ds(y, 8), pl.ds(z, 8), :] = near.reshape(1, 8, 8, wide)

    def weights(ref, code):
        return jnp.concatenate([ref[code], ref[9 + code], ref[18 + code]], 0)

    hidden_pre = None
    for code in range(9):
        dy, dz = divmod(code, 3)
        shifted = masked_w[:, 6 + dy : 16 + dy, 6 + dz : 22 + dz, :].reshape(12 * 160, LANES).astype(BF16)
        rows = jnp.concatenate([shifted[160 * dx : 160 * dx + 1600] for dx in range(3)], 1)
        term = jnp.dot(rows, weights(one_ref, code), preferred_element_type=F32)
        hidden_pre = term if hidden_pre is None else hidden_pre + term
    flags = masked_w[1:11, 7:17, 7:23, channels : channels + 1].reshape(1600, 1) > 0
    hidden_pre = jnp.where(flags, hidden_pre, 0.0)
    hidden = hidden_pre * jax.nn.sigmoid(hidden_pre)
    hidden_w[..., :channels] = hidden.reshape(10, 10, 16, channels)
    hidden_w[..., channels:] = jnp.zeros((10, 10, 16, LANES - channels), F32)
    own_pre = hidden_pre.reshape(10, 10, 16, channels)[1:9, 1:9, 1:9, :].reshape(512, channels)
    own_flag = masked_w[2:10, 8:16, 8:16, channels : channels + 1].reshape(512, 1) > 0

    rows_per_tile = outs + channels
    turned_out = jnp.where(occupancy_ref[...] > 0, cotangent_ref[...].astype(F32), 0.0).astype(BF16)
    output = None
    total[...] = jnp.zeros_like(total)
    for code in range(9):
        dy, dz = divmod(code, 3)
        shifted = hidden_w[:, dy : dy + 8, dz : dz + 8, :].reshape(640, LANES).astype(BF16)
        rows = jnp.concatenate([shifted[64 * dx : 64 * dx + 512] for dx in range(3)], 1)
        term = jnp.dot(rows, weights(two_ref, code), preferred_element_type=F32)
        output = term if output is None else output + term
        product = jnp.dot(turned_out, rows, preferred_element_type=F32)
        for dx in range(3):
            store_gradient(total, product[:, dx * LANES : (dx + 1) * LANES], 9 * dx + code, 0, rows_per_tile, channels)
    output_ref[...] = jnp.where(own_flag, output, 0.0).T.astype(BF16)

    back = None
    for code in range(9):
        dy, dz = divmod(code, 3)
        shifted = grad_w[:, 7 + dy : 15 + dy, 7 + dz : 15 + dz, :].reshape(640, wide).astype(BF16)
        rows = jnp.concatenate([shifted[64 * dx : 64 * dx + 512] for dx in range(3)], 1)
        kernel = jnp.concatenate([turned_ref[26 - code], turned_ref[17 - code], turned_ref[8 - code]], 0)
        term = jnp.dot(rows, kernel, preferred_element_type=F32)
        back = term if back is None else back + term
    gate = jax.nn.sigmoid(own_pre)
    grad_pre = jnp.where(own_flag, back * gate * (1.0 + own_pre * (1.0 - gate)), 0.0)
    turned_pre = grad_pre.T.astype(BF16)

    for code in range(9):
        dy, dz = divmod(code, 3)
        shifted = masked_w[1:11, 7 + dy : 15 + dy, 7 + dz : 15 + dz, :].reshape(640, LANES).astype(BF16)
        rows = jnp.concatenate([shifted[64 * dx : 64 * dx + 512] for dx in range(3)], 1)
        product = jnp.dot(turned_pre, rows, preferred_element_type=F32)
        for dx in range(3):
            store_gradient(
                total, product[:, dx * LANES : (dx + 1) * LANES], 9 * dx + code, outs, rows_per_tile, channels
            )

    half = kept_ref.shape[0]
    kept_ref[...] = total[pl.ds(pl.multiple_of(split * half, 16), half), :]
    sent_ref[...] = total[pl.ds(pl.multiple_of((1 - split) * half, 16), half), :].astype(BF16)


def unpack_kernel(sums_ref, one_ref, two_ref):
    count, channels, outs = two_ref.shape
    rows = outs + channels
    for place in range(3):
        tile = sums_ref[place * rows : (place + 1) * rows, :].astype(F32)
        for ref, part in ((two_ref, tile[:outs].T), (one_ref, tile[outs:].T)):
            spare = LANES - channels
            ref[place] = part[:channels]
            ref[3, place * spare : (place + 1) * spare, :] = part[channels:]


def call(kernel, out_shape, args, scalars=0, scratch=(), cost=None):
    specs = [pl.BlockSpec(memory_space=pltpu.SMEM)] * scalars + whole(len(args) - scalars)
    return pl.pallas_call(
        kernel,
        out_shape=out_shape,
        in_specs=specs,
        out_specs=jax.tree.map(lambda _: pl.BlockSpec(memory_space=pltpu.VMEM), out_shape),
        scratch_shapes=list(scratch),
        compiler_params=pltpu.CompilerParams(vmem_limit_bytes=VMEM_BYTES),
        cost_estimate=cost,
    )(*args)


def exchanged(value, axis, mask):
    return lax.ppermute(value, axis, [(i, i ^ mask) for i in range(lax.axis_size(axis))])


def halves(value, bit):
    half = value.shape[0] // 2
    return (
        lax.dynamic_slice_in_dim(value, bit * half, half, 0),
        lax.dynamic_slice_in_dim(value, (1 - bit) * half, half, 0),
    )


def shards(features, kernel_one, kernel_two, occupancy, neighbors, cotangent):
    channels, voxels = features.shape
    offsets, _, outs = kernel_two.shape
    regions = lax.axis_size("region")
    region = lax.axis_index("region").astype(jnp.int32)
    split = lax.axis_index("split").astype(jnp.int32)
    odd = region % 2
    position = jnp.stack([odd, split])
    wide = up_to(outs, LANES)
    struct = jax.ShapeDtypeStruct

    packed = call(pack_kernel, struct((voxels, LANES + wide), BF16), (features, occupancy, cotangent))
    partner = exchanged(packed, "split", 1)
    faces = struct((2, 128, 2 * LANES), BF16)
    first, second = call(planes_kernel, (faces, faces), (position, packed, partner), scalars=1)
    first = lax.ppermute(first, "region", [(i, i ^ 1) for i in range(regions)])
    pairs = [(i, i + 1) for i in range(1, regions - 1, 2)]
    second = lax.ppermute(second, "region", pairs + [(b, a) for a, b in pairs])
    weights = call(
        weights_kernel,
        (
            struct((offsets, LANES, channels), BF16),
            struct((offsets, LANES, outs), BF16),
            struct((offsets, wide, channels), BF16),
        ),
        (kernel_one, kernel_two),
        cost=pl.CostEstimate(flops=10**8, bytes_accessed=10**7, transcendentals=0),
    )

    groups = -(-offsets // 4)
    tile_rows = outs + channels
    rows = up_to(3 * groups * tile_rows, 2 * regions * 16)
    output, kept, sent = call(
        main_kernel,
        (struct((outs, voxels), BF16), struct((rows // 2, LANES), F32), struct((rows // 2, LANES), BF16)),
        (position, neighbors, packed, partner, first, second, cotangent, occupancy, *weights),
        scalars=2,
        scratch=(
            pltpu.VMEM((12, 24, 24, LANES), F32),
            pltpu.VMEM((10, 24, 24, wide), F32),
            pltpu.VMEM((10, 10, 16, LANES), F32),
            pltpu.VMEM((rows, LANES), F32),
        ),
    )

    total = kept + exchanged(sent, "split", 1).astype(F32)
    masks = [1 << i for i in range((regions - 1).bit_length())]
    for mask in masks:
        keep, give = halves(total, (region // mask) % 2)
        total = keep + exchanged(give.astype(BF16), "region", mask).astype(F32)
    total = total.astype(BF16)
    for axis, mask in [("region", mask) for mask in reversed(masks)] + [("split", 1)]:
        other = exchanged(total, axis, mask)
        bit = (region // mask) % 2 if axis == "region" else split
        total = jnp.where(bit == 0, jnp.concatenate([total, other], 0), jnp.concatenate([other, total], 0))

    grad_one, grad_two = pl.pallas_call(
        unpack_kernel,
        grid=(groups,),
        in_specs=[pl.BlockSpec((3 * tile_rows, LANES), lambda i: (i, 0))],
        out_specs=[
            pl.BlockSpec((4, channels, channels), lambda i: (i, 0, 0)),
            pl.BlockSpec((4, channels, outs), lambda i: (i, 0, 0)),
        ],
        out_shape=[struct((offsets, channels, channels), F32), struct((offsets, channels, outs), F32)],
    )(total)
    return output, grad_one, grad_two


def solution(mesh):
    rows = P(("region", "split"), None)
    columns = P(None, ("region", "split"))
    return jax.shard_map(
        shards,
        mesh=mesh,
        in_specs=(columns, P(), P(), rows, rows, columns),
        out_specs=(columns, P(), P()),
        check_vma=False,
    )
```

```python
import jax
import jax.numpy as jnp
from jax import lax
from jax.experimental import pallas as pl
from jax.experimental.pallas import tpu as pltpu
from jax.sharding import PartitionSpec as P

F32 = jnp.float32
BF16 = jnp.bfloat16
LANES = 128
VMEM_BYTES = 56 * 2**20


def up_to(value, step):
    return -(-value // step) * step


def whole(count):
    return [pl.BlockSpec(memory_space=pltpu.VMEM)] * count


def pack_kernel(features_ref, occupancy_ref, cotangent_ref, packed_ref):
    channels, voxels = features_ref.shape
    outs = cotangent_ref.shape[0]
    active = occupancy_ref[...] > 0
    masked = jnp.where(active, features_ref[...].astype(F32), 0.0)
    flag = jnp.where(active, 1.0, 0.0)
    row = lax.broadcasted_iota(jnp.int32, (LANES - channels, voxels), 0)
    tail = jnp.where(row == 0, jnp.broadcast_to(flag, row.shape), 0.0)
    packed_ref[:, :LANES] = jnp.concatenate([masked, tail], 0).T.astype(BF16)
    grad_out = jnp.where(active, cotangent_ref[...].astype(F32), 0.0)
    spare = up_to(outs, LANES) - outs
    grad_out = jnp.concatenate([grad_out, jnp.zeros((spare, voxels), F32)], 0)
    packed_ref[:, LANES:] = grad_out.T.astype(BF16)


def planes_kernel(position_ref, own_ref, partner_ref, first_ref, second_ref):
    odd = position_ref[0]
    for which, target in enumerate((first_ref, second_ref)):
        upper = 1 - odd if which == 0 else odd
        for source, block in enumerate((own_ref, partner_ref)):
            row = pl.multiple_of(upper * 384, 128)
            near = pl.multiple_of(upper * 448, 64)
            target[source, :, :LANES] = block[pl.ds(row, 128), :LANES]
            target[source, :64, LANES:] = block[pl.ds(near, 64), LANES : 2 * LANES]
            target[source, 64:, LANES:] = block[pl.ds(near, 64), 2 * LANES :]


def weights_kernel(one_ref, two_ref, one_pad_ref, two_pad_ref, two_turned_ref):
    offsets, channels, outs = two_ref.shape
    one_pad_ref[:, :channels, :] = one_ref[...]
    two_pad_ref[:, :channels, :] = two_ref[...]
    spare = LANES - channels
    one_pad_ref[:, channels:, :] = jnp.zeros((offsets, spare, one_ref.shape[2]), BF16)
    two_pad_ref[:, channels:, :] = jnp.zeros((offsets, spare, outs), BF16)
    two_turned_ref[:, outs:, :] = jnp.zeros((offsets, two_turned_ref.shape[1] - outs, channels), BF16)
    for offset in range(offsets):
        two_turned_ref[offset, :outs, :] = two_ref[offset].astype(F32).T.astype(BF16)


def store_gradient(total_ref, product, offset, first_row, rows, channels):
    group, place = divmod(offset, 4)
    if place < 3:
        base = (3 * group + place) * rows + first_row
        total_ref[base : base + product.shape[0], :channels] = product[:, :channels]
    else:
        spare = LANES - channels
        for piece in range(3):
            base = (3 * group + piece) * rows + first_row
            total_ref[base : base + product.shape[0], channels:] = product[:, piece * spare : (piece + 1) * spare]


def main_kernel(
    position_ref, neighbors_ref, own_ref, partner_ref, first_ref, second_ref, cotangent_ref, occupancy_ref,
    one_ref, two_ref, turned_ref, output_ref, kept_ref, sent_ref, masked_w, grad_w, hidden_w, total,
):
    odd, split = position_ref[0], position_ref[1]
    channels = one_ref.shape[2]
    outs = two_ref.shape[2]
    wide = grad_w.shape[3]
    masked_w[:, 6:18] = jnp.zeros((12, 12, 24, LANES), F32)
    grad_w[:, 7:17] = jnp.zeros((10, 10, 24, wide), F32)

    own = own_ref[...].astype(F32).reshape(8, 8, 8, LANES + wide)
    masked_w[2:10, 8:16, 8:16, :] = own[..., :LANES]
    grad_w[1:9, 8:16, 8:16, :] = own[..., LANES:]

    def placed(step_x, step_z):
        found = [neighbors_ref[0, 9 * (step_x + 1) + 3 * step_y + step_z + 1] >= 0 for step_y in range(3)]
        y = jnp.where(found[0], 0, jnp.where(found[1], 1, 2))
        return found[0] | found[1] | found[2], pl.multiple_of(8 * y, 8)

    step_z = 1 - 2 * split
    valid, y = placed(0, step_z)
    z = pl.multiple_of(8 + 8 * step_z, 8)

    @pl.when(valid)
    def _():
        block = partner_ref[...].astype(F32).reshape(8, 8, 8, LANES + wide)
        masked_w[2:10, pl.ds(y, 8), pl.ds(z, 8), :] = block[..., :LANES]
        grad_w[1:9, pl.ds(y, 8), pl.ds(z, 8), :] = block[..., LANES:]

    for which, ref in enumerate((first_ref, second_ref)):
        step_x = 1 - 2 * odd if which == 0 else 2 * odd - 1
        for source in range(2):
            step_z = 0 if source == 0 else 1 - 2 * split
            valid, y = placed(step_x, step_z)
            z = pl.multiple_of(8 + 8 * step_z, 8)
            x_masked = jnp.where(step_x > 0, 10, 0)
            x_grad = jnp.where(step_x > 0, 9, 0)

            @pl.when(valid)
            def _():
                block = ref[source].astype(F32)
                masked_w[pl.ds(x_masked, 2), pl.ds(y, 8), pl.ds(z, 8), :] = block[:, :LANES].reshape(2, 8, 8, LANES)
                near = jnp.concatenate([block[:64, LANES:], block[64:, LANES:]], 1)
                grad_w[pl.ds(x_grad, 1), pl.ds(y, 8), pl.ds(z, 8), :] = near.reshape(1, 8, 8, wide)

    def weights(ref, code):
        return jnp.concatenate([ref[code], ref[9 + code], ref[18 + code]], 0)

    hidden_pre = None
    for code in range(9):
        dy, dz = divmod(code, 3)
        shifted = masked_w[:, 6 + dy : 16 + dy, 6 + dz : 22 + dz, :].reshape(12 * 160, LANES).astype(BF16)
        rows = jnp.concatenate([shifted[160 * dx : 160 * dx + 1600] for dx in range(3)], 1)
        term = jnp.dot(rows, weights(one_ref, code), preferred_element_type=F32)
        hidden_pre = term if hidden_pre is None else hidden_pre + term
    flags = masked_w[1:11, 7:17, 7:23, channels : channels + 1].reshape(1600, 1) > 0
    hidden_pre = jnp.where(flags, hidden_pre, 0.0)
    hidden = hidden_pre * jax.nn.sigmoid(hidden_pre)
    hidden_w[..., :channels] = hidden.reshape(10, 10, 16, channels)
    hidden_w[..., channels:] = jnp.zeros((10, 10, 16, LANES - channels), F32)
    own_pre = hidden_pre.reshape(10, 10, 16, channels)[1:9, 1:9, 1:9, :].reshape(512, channels)
    own_flag = masked_w[2:10, 8:16, 8:16, channels : channels + 1].reshape(512, 1) > 0

    third = kept_ref.shape[1]
    first_one = 4 * third
    turned_out = jnp.where(occupancy_ref[...] > 0, cotangent_ref[...].astype(F32), 0.0).astype(BF16)
    output = None
    total[...] = jnp.zeros_like(total)
    for code in range(9):
        dy, dz = divmod(code, 3)
        shifted = hidden_w[:, dy : dy + 8, dz : dz + 8, :].reshape(640, LANES).astype(BF16)
        rows = jnp.concatenate([shifted[64 * dx : 64 * dx + 512] for dx in range(3)], 1)
        term = jnp.dot(rows, weights(two_ref, code), preferred_element_type=F32)
        output = term if output is None else output + term
        product = jnp.dot(turned_out, rows, preferred_element_type=F32)
        for dx in range(3):
            store_gradient(total, product[:, dx * LANES : (dx + 1) * LANES], 9 * dx + code, 0, outs, channels)
    output_ref[...] = jnp.where(own_flag, output, 0.0).T.astype(BF16)

    back = None
    for code in range(9):
        dy, dz = divmod(code, 3)
        shifted = grad_w[:, 7 + dy : 15 + dy, 7 + dz : 15 + dz, :].reshape(640, wide).astype(BF16)
        rows = jnp.concatenate([shifted[64 * dx : 64 * dx + 512] for dx in range(3)], 1)
        kernel = jnp.concatenate([turned_ref[26 - code], turned_ref[17 - code], turned_ref[8 - code]], 0)
        term = jnp.dot(rows, kernel, preferred_element_type=F32)
        back = term if back is None else back + term
    gate = jax.nn.sigmoid(own_pre)
    grad_pre = jnp.where(own_flag, back * gate * (1.0 + own_pre * (1.0 - gate)), 0.0)
    turned_pre = grad_pre.T.astype(BF16)

    for code in range(9):
        dy, dz = divmod(code, 3)
        shifted = masked_w[1:11, 7 + dy : 15 + dy, 7 + dz : 15 + dz, :].reshape(640, LANES).astype(BF16)
        rows = jnp.concatenate([shifted[64 * dx : 64 * dx + 512] for dx in range(3)], 1)
        product = jnp.dot(turned_pre, rows, preferred_element_type=F32)
        for dx in range(3):
            store_gradient(
                total, product[:, dx * LANES : (dx + 1) * LANES], 9 * dx + code, first_one, channels, channels
            )

    for group in range(3):
        start = 2 * third * group
        kept_ref[group] = total[pl.ds(pl.multiple_of(start + split * third, 16), third), :]
        sent_ref[group] = total[pl.ds(pl.multiple_of(start + (1 - split) * third, 16), third), :].astype(BF16)


def unpack_kernel(two_sums_ref, one_sums_ref, one_ref, two_ref):
    for sums, ref in ((two_sums_ref, two_ref), (one_sums_ref, one_ref)):
        channels, outs = ref.shape[1:]
        spare = LANES - channels
        for place in range(3):
            part = sums[place * outs : (place + 1) * outs, :].astype(F32).T
            ref[place] = part[:channels]
            ref[3, place * spare : (place + 1) * spare, :] = part[channels:]


def call(kernel, out_shape, args, scalars=0, scratch=(), cost=None):
    specs = [pl.BlockSpec(memory_space=pltpu.SMEM)] * scalars + whole(len(args) - scalars)
    return pl.pallas_call(
        kernel,
        out_shape=out_shape,
        in_specs=specs,
        out_specs=jax.tree.map(lambda _: pl.BlockSpec(memory_space=pltpu.VMEM), out_shape),
        scratch_shapes=list(scratch),
        compiler_params=pltpu.CompilerParams(vmem_limit_bytes=VMEM_BYTES),
        cost_estimate=cost,
    )(*args)


def exchanged(value, axis, mask):
    return lax.ppermute(value, axis, [(i, i ^ mask) for i in range(lax.axis_size(axis))])


def halves(value, bit):
    half = value.shape[0] // 2
    return (
        lax.dynamic_slice_in_dim(value, bit * half, half, 0),
        lax.dynamic_slice_in_dim(value, (1 - bit) * half, half, 0),
    )


def shards(features, kernel_one, kernel_two, occupancy, neighbors, cotangent):
    channels, voxels = features.shape
    offsets, _, outs = kernel_two.shape
    regions = lax.axis_size("region")
    region = lax.axis_index("region").astype(jnp.int32)
    split = lax.axis_index("split").astype(jnp.int32)
    odd = region % 2
    position = jnp.stack([odd, split])
    wide = up_to(outs, LANES)
    struct = jax.ShapeDtypeStruct

    packed = call(pack_kernel, struct((voxels, LANES + wide), BF16), (features, occupancy, cotangent))
    partner = exchanged(packed, "split", 1)
    faces = struct((2, 128, 2 * LANES), BF16)
    first, second = call(planes_kernel, (faces, faces), (position, packed, partner), scalars=1)
    first = lax.ppermute(first, "region", [(i, i ^ 1) for i in range(regions)])
    pairs = [(i, i + 1) for i in range(1, regions - 1, 2)]
    second = lax.ppermute(second, "region", pairs + [(b, a) for a, b in pairs])
    weights = call(
        weights_kernel,
        (
            struct((offsets, LANES, channels), BF16),
            struct((offsets, LANES, outs), BF16),
            struct((offsets, wide, channels), BF16),
        ),
        (kernel_one, kernel_two),
        cost=pl.CostEstimate(flops=10**8, bytes_accessed=10**7, transcendentals=0),
    )

    fours = -(-offsets // 4)
    third = up_to(3 * fours * channels, 2 * regions * 8) // 2
    output, kept, sent = call(
        main_kernel,
        (struct((outs, voxels), BF16), struct((3, third, LANES), F32), struct((3, third, LANES), BF16)),
        (position, neighbors, packed, partner, first, second, cotangent, occupancy, *weights),
        scalars=2,
        scratch=(
            pltpu.VMEM((12, 24, 24, LANES), F32),
            pltpu.VMEM((10, 24, 24, wide), F32),
            pltpu.VMEM((10, 10, 16, LANES), F32),
            pltpu.VMEM((6 * third, LANES), F32),
        ),
    )

    received = exchanged(sent, "split", 1).astype(F32)
    sums = [kept[part] + received[part] for part in range(3)]
    bits = list(range((regions - 1).bit_length()))
    orders = [bits, bits[1::-1] + bits[2:], bits[2:] + bits[:2]]

    for step in range(len(bits) - 1):
        for part, order in enumerate(orders):
            mask = 1 << order[step]
            keep, give = halves(sums[part], (region // mask) % 2)
            sums[part] = keep + exchanged(give.astype(BF16), "region", mask).astype(F32)
    for part, order in enumerate(orders):
        own = sums[part].astype(BF16)
        sums[part] = (own.astype(F32) + exchanged(own, "region", 1 << order[-1]).astype(F32)).astype(BF16)

    def joined(own, other, bit):
        return jnp.where(bit == 0, jnp.concatenate([own, other], 0), jnp.concatenate([other, own], 0))

    for step in reversed(range(len(bits) - 1)):
        for part, order in enumerate(orders):
            mask = 1 << order[step]
            sums[part] = joined(sums[part], exchanged(sums[part], "region", mask), (region // mask) % 2)
    other = exchanged(jnp.stack(sums), "split", 1)
    sums = [joined(sums[part], other[part], split) for part in range(3)]

    grad_one, grad_two = pl.pallas_call(
        unpack_kernel,
        grid=(fours,),
        in_specs=[
            pl.BlockSpec((3 * outs, LANES), lambda i: (i, 0)),
            pl.BlockSpec((3 * channels, LANES), lambda i: (i, 0)),
        ],
        out_specs=[
            pl.BlockSpec((4, channels, channels), lambda i: (i, 0, 0)),
            pl.BlockSpec((4, channels, outs), lambda i: (i, 0, 0)),
        ],
        out_shape=[struct((offsets, channels, channels), F32), struct((offsets, channels, outs), F32)],
    )(jnp.concatenate(sums[:2], 0), sums[2])
    return output, grad_one, grad_two


def solution(mesh):
    rows = P(("region", "split"), None)
    columns = P(None, ("region", "split"))
    return jax.shard_map(
        shards,
        mesh=mesh,
        in_specs=(columns, P(), P(), rows, rows, columns),
        out_specs=(columns, P(), P()),
        check_vma=False,
    )
```

```python
import jax
import jax.numpy as jnp
from jax import lax
from jax.experimental import pallas as pl
from jax.experimental.pallas import tpu as pltpu
from jax.sharding import PartitionSpec as P

F32 = jnp.float32
BF16 = jnp.bfloat16
LANES = 128
VMEM_BYTES = 32 * 2**20


def up_to(value, step):
    return -(-value // step) * step


def whole(count):
    return [pl.BlockSpec(memory_space=pltpu.VMEM)] * count


def pack_kernel(position_ref, features_ref, occupancy_ref, cotangent_ref, packed_ref, first_ref, second_ref):
    channels, voxels = features_ref.shape
    outs = cotangent_ref.shape[0]
    active = occupancy_ref[...] > 0
    masked = jnp.where(active, features_ref[...].astype(F32), 0.0)
    flag = jnp.where(active, 1.0, 0.0)
    row = lax.broadcasted_iota(jnp.int32, (LANES - channels, voxels), 0)
    tail = jnp.where(row == 0, jnp.broadcast_to(flag, row.shape), 0.0)
    packed_ref[:, :LANES] = jnp.concatenate([masked, tail], 0).T.astype(BF16)
    grad_out = jnp.where(active, cotangent_ref[...].astype(F32), 0.0)
    spare = up_to(outs, LANES) - outs
    grad_out = jnp.concatenate([grad_out, jnp.zeros((spare, voxels), F32)], 0)
    packed_ref[:, LANES:] = grad_out.T.astype(BF16)
    odd = position_ref[0]
    for target, upper in ((first_ref, 1 - odd), (second_ref, odd)):
        row = pl.multiple_of(upper * 384, 128)
        near = pl.multiple_of(upper * 448, 64)
        target[:, :LANES] = packed_ref[pl.ds(row, 128), :LANES]
        target[:64, LANES:] = packed_ref[pl.ds(near, 64), LANES : 2 * LANES]
        target[64:, LANES:] = packed_ref[pl.ds(near, 64), 2 * LANES :]


def weights_kernel(one_ref, two_ref, one_pad_ref, two_pad_ref):
    offsets, channels, outs = two_ref.shape
    spare = LANES - channels
    one_pad_ref[:, :channels, :] = one_ref[...]
    one_pad_ref[:, channels:, :] = jnp.zeros((offsets, spare, one_ref.shape[2]), BF16)
    two_pad_ref[:, :channels, :outs] = two_ref[...]
    two_pad_ref[:, :channels, outs:] = jnp.zeros((offsets, channels, two_pad_ref.shape[2] - outs), BF16)
    two_pad_ref[:, channels:, :] = jnp.zeros((offsets, spare, two_pad_ref.shape[2]), BF16)


def store_two(total_ref, product, offset):
    rows, outs = product.shape
    spare = outs - LANES
    pair, place = divmod(offset, 2)
    total_ref[pl.ds((3 * pair + place) * rows, rows), :] = product[:, :LANES]
    total_ref[pl.ds((3 * pair + 2) * rows, rows), place * spare : (place + 1) * spare] = product[:, LANES:]


def store_one(total_ref, product, offset, first_row):
    rows, channels = product.shape
    spare = LANES - channels
    group, place = divmod(offset, 4)
    if place < 3:
        total_ref[pl.ds(first_row + (3 * group + place) * rows, rows), :channels] = product
    else:
        for piece in range(3):
            base = first_row + (3 * group + piece) * rows
            total_ref[pl.ds(base, rows), channels:] = product[:, piece * spare : (piece + 1) * spare]


def main_kernel(
    position_ref, neighbors_ref, own_ref, partner_ref, first_ref, second_ref, first_far_ref, second_far_ref,
    one_ref, two_ref, output_ref, kept_ref, sent_ref, masked_w, grad_w, hidden_w, total,
):
    odd, split = position_ref[0], position_ref[1]
    channels = one_ref.shape[2]
    outs = output_ref.shape[0]
    wide = grad_w.shape[3]
    over = (((0,), (0,)), ((), ()))
    masked_w[:, 6:18] = jnp.zeros((12, 12, 24, LANES), F32)
    grad_w[:, 7:17] = jnp.zeros((10, 10, 24, wide), F32)

    own = own_ref[...].astype(F32).reshape(8, 8, 8, LANES + wide)
    masked_w[2:10, 8:16, 8:16, :] = own[..., :LANES]
    grad_w[1:9, 8:16, 8:16, :] = own[..., LANES:]

    def placed(step_x, step_z):
        found = [neighbors_ref[0, 9 * (step_x + 1) + 3 * step_y + step_z + 1] >= 0 for step_y in range(3)]
        y = jnp.where(found[0], 0, jnp.where(found[1], 1, 2))
        return found[0] | found[1] | found[2], pl.multiple_of(8 * y, 8)

    step_z = 1 - 2 * split
    valid, y = placed(0, step_z)
    z = pl.multiple_of(8 + 8 * step_z, 8)

    @pl.when(valid)
    def _():
        block = partner_ref[...].astype(F32).reshape(8, 8, 8, LANES + wide)
        masked_w[2:10, pl.ds(y, 8), pl.ds(z, 8), :] = block[..., :LANES]
        grad_w[1:9, pl.ds(y, 8), pl.ds(z, 8), :] = block[..., LANES:]

    for which, refs in enumerate(((first_ref, first_far_ref), (second_ref, second_far_ref))):
        step_x = 1 - 2 * odd if which == 0 else 2 * odd - 1
        for source, ref in enumerate(refs):
            step_z = 0 if source == 0 else 1 - 2 * split
            valid, y = placed(step_x, step_z)
            z = pl.multiple_of(8 + 8 * step_z, 8)
            x_masked = jnp.where(step_x > 0, 10, 0)
            x_grad = jnp.where(step_x > 0, 9, 0)

            @pl.when(valid)
            def _():
                block = ref[...].astype(F32)
                masked_w[pl.ds(x_masked, 2), pl.ds(y, 8), pl.ds(z, 8), :] = block[:, :LANES].reshape(2, 8, 8, LANES)
                near = jnp.concatenate([block[:64, LANES:], block[64:, LANES:]], 1)
                grad_w[pl.ds(x_grad, 1), pl.ds(y, 8), pl.ds(z, 8), :] = near.reshape(1, 8, 8, wide)

    def weights(ref, code):
        return jnp.concatenate([ref[code], ref[9 + code], ref[18 + code]], 0)

    hidden_pre = None
    for code in range(9):
        dy, dz = divmod(code, 3)
        shifted = masked_w[:, 6 + dy : 16 + dy, 6 + dz : 22 + dz, :].reshape(12 * 160, LANES).astype(BF16)
        rows = jnp.concatenate([shifted[160 * dx : 160 * dx + 1600] for dx in range(3)], 1)
        term = jnp.dot(rows, weights(one_ref, code), preferred_element_type=F32)
        hidden_pre = term if hidden_pre is None else hidden_pre + term
    flags = masked_w[1:11, 7:17, 7:23, channels : channels + 1].reshape(1600, 1) > 0
    hidden_pre = jnp.where(flags, hidden_pre, 0.0)
    hidden = hidden_pre * jax.nn.sigmoid(hidden_pre)
    hidden_w[..., :channels] = hidden.reshape(10, 10, 16, channels)
    hidden_w[..., channels:] = jnp.zeros((10, 10, 16, LANES - channels), F32)
    own_pre = hidden_pre.reshape(10, 10, 16, channels)[1:9, 1:9, 1:9, :].reshape(512, channels)
    own_flag = masked_w[2:10, 8:16, 8:16, channels : channels + 1].reshape(512, 1) > 0

    third = kept_ref.shape[1]
    grad_out = own_ref[:, LANES : LANES + outs]
    output = None
    total[...] = jnp.zeros_like(total)
    for code in range(9):
        dy, dz = divmod(code, 3)
        shifted = hidden_w[:, dy : dy + 8, dz : dz + 8, :].reshape(640, LANES).astype(BF16)
        rows = jnp.concatenate([shifted[64 * dx : 64 * dx + 512] for dx in range(3)], 1)
        term = jnp.dot(rows, weights(two_ref, code)[:, :outs], preferred_element_type=F32)
        output = term if output is None else output + term
        product = lax.dot_general(rows, grad_out, over, preferred_element_type=F32)
        for dx in range(3):
            store_two(total, product[dx * LANES : dx * LANES + channels], 9 * dx + code)
    output_ref[...] = jnp.where(own_flag, output, 0.0).T.astype(BF16)

    back = None
    for code in range(9):
        dy, dz = divmod(code, 3)
        shifted = grad_w[:, 7 + dy : 15 + dy, 7 + dz : 15 + dz, :].reshape(640, wide).astype(BF16)
        rows = jnp.concatenate([shifted[64 * dx : 64 * dx + 512] for dx in range(3)], 1)
        kernel = jnp.concatenate([two_ref[26 - code], two_ref[17 - code], two_ref[8 - code]], 1)
        term = lax.dot_general(rows, kernel, (((1,), (1,)), ((), ())), preferred_element_type=F32)
        back = term if back is None else back + term
    back = back[:, :channels]
    gate = jax.nn.sigmoid(own_pre)
    grad_pre = jnp.where(own_flag, back * gate * (1.0 + own_pre * (1.0 - gate)), 0.0).astype(BF16)

    for code in range(9):
        dy, dz = divmod(code, 3)
        shifted = masked_w[1:11, 7 + dy : 15 + dy, 7 + dz : 15 + dz, :].reshape(640, LANES).astype(BF16)
        rows = jnp.concatenate([shifted[64 * dx : 64 * dx + 512] for dx in range(3)], 1)
        product = lax.dot_general(rows, grad_pre, over, preferred_element_type=F32)
        for dx in range(3):
            store_one(total, product[dx * LANES : dx * LANES + channels], 9 * dx + code, 4 * third)

    for group in range(3):
        start = 2 * third * group
        kept_ref[group] = total[pl.ds(pl.multiple_of(start + split * third, 16), third), :]
        sent_ref[group] = total[pl.ds(pl.multiple_of(start + (1 - split) * third, 16), third), :].astype(BF16)


def unpack_kernel(position_ref, own_ref, other_ref, one_ref, two_ref, sums):
    split = position_ref[1]
    offsets, channels, outs = two_ref.shape
    third = own_ref.shape[1]
    for part in range(3):
        for place, ref in ((split, own_ref), (1 - split, other_ref)):
            sums[pl.ds(pl.multiple_of((2 * part + place) * third, 16), third), :] = ref[part]
    for offset in range(offsets):
        pair, place = divmod(offset, 2)
        base = 3 * pair * channels
        spare = outs - LANES
        two_ref[offset, :, :LANES] = sums[pl.ds(base + place * channels, channels), :].astype(F32)
        two_ref[offset, :, LANES:] = sums[pl.ds(base + 2 * channels, channels), :].astype(F32)[
            :, place * spare : (place + 1) * spare
        ]
    for offset in range(offsets):
        group, place = divmod(offset, 4)
        base = 4 * third + 3 * group * channels
        spare = LANES - channels
        if place < 3:
            one_ref[offset] = sums[pl.ds(base + place * channels, channels), :].astype(F32)[:, :channels]
        else:
            for piece in range(3):
                one_ref[offset, :, piece * spare : (piece + 1) * spare] = sums[
                    pl.ds(base + piece * channels, channels), :
                ].astype(F32)[:, channels:]


def call(kernel, out_shape, args, scalars=0, scratch=(), cost=None):
    specs = [pl.BlockSpec(memory_space=pltpu.SMEM)] * scalars + whole(len(args) - scalars)
    return pl.pallas_call(
        kernel,
        out_shape=out_shape,
        in_specs=specs,
        out_specs=jax.tree.map(lambda _: pl.BlockSpec(memory_space=pltpu.VMEM), out_shape),
        scratch_shapes=list(scratch),
        compiler_params=pltpu.CompilerParams(vmem_limit_bytes=VMEM_BYTES),
        cost_estimate=cost,
    )(*args)


def exchanged(value, axis, mask):
    return lax.ppermute(value, axis, [(i, i ^ mask) for i in range(lax.axis_size(axis))])


def halves(value, bit):
    half = value.shape[0] // 2
    return (
        lax.dynamic_slice_in_dim(value, bit * half, half, 0),
        lax.dynamic_slice_in_dim(value, (1 - bit) * half, half, 0),
    )


def shards(features, kernel_one, kernel_two, occupancy, neighbors, cotangent):
    channels, voxels = features.shape
    offsets, _, outs = kernel_two.shape
    regions = lax.axis_size("region")
    region = lax.axis_index("region").astype(jnp.int32)
    split = lax.axis_index("split").astype(jnp.int32)
    odd = region % 2
    position = jnp.stack([odd, split])
    wide = up_to(outs, LANES)
    struct = jax.ShapeDtypeStruct

    planes = struct((128, 2 * LANES), BF16)
    packed, first, second = call(
        pack_kernel,
        (struct((voxels, LANES + wide), BF16), planes, planes),
        (position, features, occupancy, cotangent),
        scalars=1,
    )
    partner = exchanged(packed, "split", 1)
    first = lax.ppermute(first, "region", [(i, i ^ 1) for i in range(regions)])
    pairs = [(i, i + 1) for i in range(1, regions - 1, 2)]
    second = lax.ppermute(second, "region", pairs + [(b, a) for a, b in pairs])
    first_far, second_far = exchanged(first, "split", 1), exchanged(second, "split", 1)
    weights = call(
        weights_kernel,
        (struct((offsets, LANES, channels), BF16), struct((offsets, LANES, wide), BF16)),
        (kernel_one, kernel_two),
        cost=pl.CostEstimate(flops=10**8, bytes_accessed=10**7, transcendentals=0),
    )

    fours = -(-offsets // 4)
    third = up_to(3 * fours * channels, 2 * regions * 8) // 2
    output, kept, sent = call(
        main_kernel,
        (struct((outs, voxels), BF16), struct((3, third, LANES), F32), struct((3, third, LANES), BF16)),
        (position, neighbors, packed, partner, first, second, first_far, second_far, *weights),
        scalars=2,
        scratch=(
            pltpu.VMEM((12, 24, 24, LANES), F32),
            pltpu.VMEM((10, 24, 24, wide), F32),
            pltpu.VMEM((10, 10, 16, LANES), F32),
            pltpu.VMEM((6 * third, LANES), F32),
        ),
    )

    received = exchanged(sent, "split", 1).astype(F32)
    sums = [kept[part] + received[part] for part in range(3)]
    bits = list(range((regions - 1).bit_length()))
    orders = [bits, bits[1::-1] + bits[2:], bits[2:] + bits[:2]]

    for step in range(len(bits) - 1):
        for part, order in enumerate(orders):
            mask = 1 << order[step]
            keep, give = halves(sums[part], (region // mask) % 2)
            sums[part] = keep + exchanged(give.astype(BF16), "region", mask).astype(F32)
    for part, order in enumerate(orders):
        own = sums[part].astype(BF16)
        sums[part] = (own.astype(F32) + exchanged(own, "region", 1 << order[-1]).astype(F32)).astype(BF16)

    def joined(own, other, bit):
        return jnp.where(bit == 0, jnp.concatenate([own, other], 0), jnp.concatenate([other, own], 0))

    for step in reversed(range(len(bits) - 1)):
        for part, order in enumerate(orders):
            mask = 1 << order[step]
            sums[part] = joined(sums[part], exchanged(sums[part], "region", mask), (region // mask) % 2)
    own = jnp.stack(sums)
    grad_one, grad_two = call(
        unpack_kernel,
        (struct((offsets, channels, channels), F32), struct((offsets, channels, outs), F32)),
        (position, own, exchanged(own, "split", 1)),
        scalars=1,
        scratch=(pltpu.VMEM((6 * third, LANES), BF16),),
    )
    return output, grad_one, grad_two


def solution(mesh):
    rows = P(("region", "split"), None)
    columns = P(None, ("region", "split"))
    return jax.shard_map(
        shards,
        mesh=mesh,
        in_specs=(columns, P(), P(), rows, rows, columns),
        out_specs=(columns, P(), P()),
        check_vma=False,
    )
```

```python
import jax
import jax.numpy as jnp
from jax import lax
from jax.experimental import pallas as pl
from jax.experimental.pallas import tpu as pltpu
from jax.sharding import PartitionSpec as P

F32 = jnp.float32
BF16 = jnp.bfloat16
LANES = 128
VMEM_BYTES = 32 * 2**20


def up_to(value, step):
    return -(-value // step) * step


def fetched(pairs, sems):
    copies = [pltpu.make_async_copy(source, target, sems.at[place]) for place, (source, target) in enumerate(pairs)]
    for copy in copies:
        copy.start()
    return copies


def pack_kernel(
    position_ref, features_hbm, occupancy_hbm, cotangent_hbm, packed_ref, first_ref, second_ref, turned_ref,
    features_ref, occupancy_ref, cotangent_ref, sems,
):
    copies = fetched(
        ((occupancy_hbm, occupancy_ref), (features_hbm, features_ref), (cotangent_hbm, cotangent_ref)), sems
    )
    channels, voxels = features_ref.shape
    outs = cotangent_ref.shape[0]
    copies[0].wait()
    copies[1].wait()
    active = occupancy_ref[...] > 0
    masked = jnp.where(active, features_ref[...].astype(F32), 0.0)
    flag = jnp.where(active, 1.0, 0.0)
    row = lax.broadcasted_iota(jnp.int32, (LANES - channels, voxels), 0)
    tail = jnp.where(row == 0, jnp.broadcast_to(flag, row.shape), 0.0)
    packed_ref[:, :LANES] = jnp.concatenate([masked, tail], 0).T.astype(BF16)
    copies[2].wait()
    grad_out = jnp.where(active, cotangent_ref[...].astype(F32), 0.0)
    turned_ref[...] = grad_out.astype(BF16)
    spare = up_to(outs, LANES) - outs
    grad_out = jnp.concatenate([grad_out, jnp.zeros((spare, voxels), F32)], 0)
    packed_ref[:, LANES:] = grad_out.T.astype(BF16)
    odd = position_ref[0]
    for target, upper in ((first_ref, 1 - odd), (second_ref, odd)):
        row = pl.multiple_of(upper * 384, 128)
        near = pl.multiple_of(upper * 448, 64)
        target[:, :LANES] = packed_ref[pl.ds(row, 128), :LANES]
        target[:64, LANES:] = packed_ref[pl.ds(near, 64), LANES : 2 * LANES]
        target[64:, LANES:] = packed_ref[pl.ds(near, 64), 2 * LANES :]


def weights_kernel(one_hbm, two_hbm, one_pad_ref, two_pad_ref, one_ref, two_ref, sems):
    copies = fetched(((one_hbm, one_ref), (two_hbm, two_ref)), sems)
    offsets, channels, outs = two_ref.shape
    spare = LANES - channels
    one_pad_ref[:, channels:, :] = jnp.zeros((offsets, spare, one_ref.shape[2]), BF16)
    copies[0].wait()
    one_pad_ref[:, :channels, :] = one_ref[...]
    copies[1].wait()
    two_pad_ref[:, :channels, :outs] = two_ref[...]
    two_pad_ref[:, :channels, outs:] = jnp.zeros((offsets, channels, two_pad_ref.shape[2] - outs), BF16)
    two_pad_ref[:, channels:, :] = jnp.zeros((offsets, spare, two_pad_ref.shape[2]), BF16)


def store_turned(total_ref, product, offset, first_row, channels):
    rows = product.shape[0]
    spare = LANES - channels
    group, place = divmod(offset, 4)
    if place < 3:
        base = first_row + (3 * group + place) * rows
        total_ref[pl.ds(base, rows), :channels] = product[:, :channels]
    else:
        for piece in range(3):
            base = first_row + (3 * group + piece) * rows
            total_ref[pl.ds(base, rows), channels:] = product[:, piece * spare : (piece + 1) * spare]


def main_kernel(
    position_ref, neighbors_ref, own_ref, partner_ref, first_ref, second_ref, first_far_ref, second_far_ref,
    turned_ref, one_ref, two_ref, output_ref, kept_p_ref, kept_q_ref, sent_p_ref, sent_q_ref, masked_w, grad_w, hidden_w, total, masked_s, plane_s, hidden_s, grad_s,
):
    odd, split = position_ref[0], position_ref[1]
    channels = one_ref.shape[2]
    outs = output_ref.shape[0]
    wide = grad_w.shape[3]
    masked_w[:, 6:18] = jnp.zeros((12, 12, 24, LANES), F32)
    grad_w[:, 7:17] = jnp.zeros((10, 10, 24, wide), F32)

    own = own_ref[...].astype(F32).reshape(8, 8, 8, LANES + wide)
    masked_w[2:10, 8:16, 8:16, :] = own[..., :LANES]
    grad_w[1:9, 8:16, 8:16, :] = own[..., LANES:]

    def placed(step_x, step_z):
        found = [neighbors_ref[0, 9 * (step_x + 1) + 3 * step_y + step_z + 1] >= 0 for step_y in range(3)]
        y = jnp.where(found[0], 0, jnp.where(found[1], 1, 2))
        return found[0] | found[1] | found[2], pl.multiple_of(8 * y, 8)

    step_z = 1 - 2 * split
    valid, y = placed(0, step_z)
    z = pl.multiple_of(8 + 8 * step_z, 8)

    @pl.when(valid)
    def _():
        block = partner_ref[...].astype(F32).reshape(8, 8, 8, LANES + wide)
        masked_w[2:10, pl.ds(y, 8), pl.ds(z, 8), :] = block[..., :LANES]
        grad_w[1:9, pl.ds(y, 8), pl.ds(z, 8), :] = block[..., LANES:]

    for which, refs in enumerate(((first_ref, first_far_ref), (second_ref, second_far_ref))):
        step_x = 1 - 2 * odd if which == 0 else 2 * odd - 1
        for source, ref in enumerate(refs):
            step_z = 0 if source == 0 else 1 - 2 * split
            valid, y = placed(step_x, step_z)
            z = pl.multiple_of(8 + 8 * step_z, 8)
            x_masked = jnp.where(step_x > 0, 10, 0)
            x_grad = jnp.where(step_x > 0, 9, 0)

            @pl.when(valid)
            def _():
                block = ref[...].astype(F32)
                masked_w[pl.ds(x_masked, 2), pl.ds(y, 8), pl.ds(z, 8), :] = block[:, :LANES].reshape(2, 8, 8, LANES)
                near = jnp.concatenate([block[:64, LANES:], block[64:, LANES:]], 1)
                grad_w[pl.ds(x_grad, 1), pl.ds(y, 8), pl.ds(z, 8), :] = near.reshape(1, 8, 8, wide)

    def stage(target, source, first_x, first_y, first_z):
        count_x, rows = target.shape[2:4]
        lanes = target.shape[4]
        for dz in range(3):
            block = source[
                first_x : first_x + count_x, first_y : first_y + rows // 8, first_z + dz : first_z + dz + 8, :
            ]
            target[dz, 0] = block.reshape(count_x, rows, lanes).astype(BF16)
            target[dz, 1, :, : rows - 16] = block[:, 1 : rows // 8 - 1].reshape(count_x, rows - 16, lanes).astype(BF16)

    def staged(target, tap, count, more=0):
        code, dx = divmod(tap, 3)
        dy, dz = divmod(code, 3)
        row = 16 * ((dy + more) // 2)
        first = dx + more
        block = target[dz, (dy + more) % 2, first : first + count, row : row + 8 * count, :]
        return block.reshape(8 * count * count, target.shape[4])

    taps = range(27)
    chunks = [taps[first : first + 6] for first in range(0, 27, 6)]

    def offset_of(tap):
        return 9 * (tap % 3) + tap // 3

    beside = 16 - 9 * split
    stage(masked_s, masked_w, 0, 6, 7)
    for dz in range(3):
        plane = masked_w[:, 6:24, pl.ds(beside - 1 + dz, 1), :].reshape(12, 18, LANES)
        for dy in range(3):
            plane_s[dz, dy] = plane[:, dy : dy + 16, :].astype(BF16)
        if dz == 1:
            plane_flag = plane[1:11, 1:17, channels : channels + 1].reshape(160, 1) > 0

    def plane_rows(tap):
        code, dx = divmod(tap, 3)
        dy, dz = divmod(code, 3)
        return plane_s[dz, dy, dx : dx + 10].reshape(160, LANES)

    hidden_pre = None
    for chunk in chunks:
        rows = jnp.concatenate(
            [jnp.concatenate([staged(masked_s, tap, 10), plane_rows(tap)], 0) for tap in chunk], 1
        )
        kernel = jnp.concatenate([one_ref[offset_of(tap)] for tap in chunk], 0)
        term = jnp.dot(rows, kernel, preferred_element_type=F32)
        hidden_pre = term if hidden_pre is None else hidden_pre + term
    flags = masked_w[1:11, 7:17, 8:16, channels : channels + 1].reshape(800, 1) > 0
    hidden_pre = jnp.where(jnp.concatenate([flags, plane_flag], 0), hidden_pre, 0.0)
    hidden = hidden_pre * jax.nn.sigmoid(hidden_pre)
    hidden = jnp.concatenate([hidden, jnp.zeros((960, LANES - channels), F32)], 1)
    hidden_w[:, :, 8:16, :] = hidden[:800].reshape(10, 10, 8, LANES)
    hidden_w[:, :, 0:8, :] = jnp.zeros((10, 10, 8, LANES), F32)
    hidden_w[:, :, 16:24, :] = jnp.zeros((10, 10, 8, LANES), F32)
    hidden_w[:, :, pl.ds(beside, 1), :] = hidden[800:].reshape(10, 16, LANES)[:, :10].reshape(10, 10, 1, LANES)
    own_pre = hidden_pre[:800].reshape(10, 10, 8, channels)[1:9, 1:9].reshape(512, channels)
    own_flag = masked_w[2:10, 8:16, 8:16, channels : channels + 1].reshape(512, 1) > 0

    first_one = 3 * (-(-27 // 4)) * outs
    turned_out = turned_ref[...]
    stage(hidden_s, hidden_w, 0, 0, 7)
    output = None
    for chunk in chunks:
        rows = jnp.concatenate([staged(hidden_s, tap, 8) for tap in chunk], 1)
        kernel = jnp.concatenate([two_ref[offset_of(tap)] for tap in chunk], 0)[:, :outs]
        term = jnp.dot(rows, kernel, preferred_element_type=F32)
        output = term if output is None else output + term
        product = jnp.dot(turned_out, rows, preferred_element_type=F32)
        for place, tap in enumerate(chunk):
            store_turned(total, product[:, place * LANES : (place + 1) * LANES], offset_of(tap), 0, channels)
    output_ref[...] = jnp.where(own_flag, output, 0.0).T.astype(BF16)

    stage(grad_s, grad_w, 0, 7, 7)
    back = None
    for chunk in chunks:
        rows = jnp.concatenate([staged(grad_s, tap, 8) for tap in chunk], 1)
        kernel = jnp.concatenate([two_ref[26 - offset_of(tap)] for tap in chunk], 1)
        term = lax.dot_general(rows, kernel, (((1,), (1,)), ((), ())), preferred_element_type=F32)
        back = term if back is None else back + term
    back = back[:, :channels]
    gate = jax.nn.sigmoid(own_pre)
    grad_pre = jnp.where(own_flag, back * gate * (1.0 + own_pre * (1.0 - gate)), 0.0)
    turned_pre = grad_pre.T.astype(BF16)

    for chunk in chunks:
        rows = jnp.concatenate([staged(masked_s, tap, 8, 1) for tap in chunk], 1)
        product = jnp.dot(turned_pre, rows, preferred_element_type=F32)
        for place, tap in enumerate(chunk):
            store_turned(
                total, product[:, place * LANES : (place + 1) * LANES], offset_of(tap), first_one, channels
            )

    half = kept_p_ref.shape[0]
    for start, kept_ref, sent_ref in ((0, kept_p_ref, sent_p_ref), (2 * half, kept_q_ref, sent_q_ref)):
        kept_ref[...] = total[pl.ds(pl.multiple_of(start + split * half, 16), half), :]
        sent_ref[...] = total[pl.ds(pl.multiple_of(start + (1 - split) * half, 16), half), :].astype(BF16)


def unpack_kernel(position_ref, own_p_ref, other_p_ref, own_q_ref, other_q_ref, one_ref, two_ref, sums):
    split = position_ref[1]
    offsets, channels, outs = two_ref.shape
    half = own_p_ref.shape[0]
    for start, own_ref, other_ref in ((0, own_p_ref, other_p_ref), (2 * half, own_q_ref, other_q_ref)):
        sums[pl.ds(pl.multiple_of(start + split * half, 16), half), :] = own_ref[...]
        sums[pl.ds(pl.multiple_of(start + (1 - split) * half, 16), half), :] = other_ref[...]
    row = lax.broadcasted_iota(jnp.int32, (LANES, LANES), 0)
    unit = jnp.where(row == lax.broadcasted_iota(jnp.int32, (LANES, LANES), 1), 1.0, 0.0).astype(BF16)
    spare = LANES - channels
    for ref, first, rows in ((two_ref, 0, outs), (one_ref, 3 * (-(-offsets // 4)) * outs, channels)):
        for tile in range(3 * (-(-offsets // 4))):
            group, place = divmod(tile, 3)
            part = sums[pl.ds(first + tile * rows, rows), :]
            part = lax.dot_general(unit, part, (((1,), (1,)), ((), ())), preferred_element_type=F32)
            ref[4 * group + place] = part[:channels]
            if 4 * group + 3 < offsets:
                ref[4 * group + 3, place * spare : (place + 1) * spare, :] = part[channels:]


def call(kernel, out_shape, args, scalars=0, scratch=(), cost=None, fetch=0, vmem=VMEM_BYTES):
    spaces = [pltpu.SMEM] * scalars + [pltpu.HBM] * fetch + [pltpu.VMEM] * (len(args) - scalars - fetch)
    return pl.pallas_call(
        kernel,
        out_shape=out_shape,
        in_specs=[pl.BlockSpec(memory_space=space) for space in spaces],
        out_specs=jax.tree.map(lambda _: pl.BlockSpec(memory_space=pltpu.VMEM), out_shape),
        scratch_shapes=list(scratch),
        compiler_params=pltpu.CompilerParams(vmem_limit_bytes=vmem),
        cost_estimate=cost,
    )(*args)


def exchanged(value, axis, mask):
    return lax.ppermute(value, axis, [(i, i ^ mask) for i in range(lax.axis_size(axis))])


def halves(value, bit):
    half = value.shape[0] // 2
    return (
        lax.dynamic_slice_in_dim(value, bit * half, half, 0),
        lax.dynamic_slice_in_dim(value, (1 - bit) * half, half, 0),
    )


def shards(features, kernel_one, kernel_two, occupancy, neighbors, cotangent):
    channels, voxels = features.shape
    offsets, _, outs = kernel_two.shape
    regions = lax.axis_size("region")
    region = lax.axis_index("region").astype(jnp.int32)
    split = lax.axis_index("split").astype(jnp.int32)
    odd = region % 2
    position = jnp.stack([odd, split])
    wide = up_to(outs, LANES)
    struct = jax.ShapeDtypeStruct

    planes = struct((128, 2 * LANES), BF16)
    packed, first, second, turned = call(
        pack_kernel,
        (struct((voxels, LANES + wide), BF16), planes, planes, struct((outs, voxels), BF16)),
        (position, features, occupancy, cotangent),
        scalars=1,
        fetch=3,
        vmem=56 * 2**20,
        scratch=(
            pltpu.VMEM(features.shape, BF16),
            pltpu.VMEM(occupancy.shape, occupancy.dtype),
            pltpu.VMEM(cotangent.shape, BF16),
            pltpu.SemaphoreType.DMA((3,)),
        ),
    )
    pairs = [(i, i + 1) for i in range(1, regions - 1, 2)]
    second = lax.ppermute(second, "region", pairs + [(b, a) for a, b in pairs])
    first = lax.ppermute(first, "region", [(i, i ^ 1) for i in range(regions)])
    partner = exchanged(packed, "split", 1)
    weights = call(
        weights_kernel,
        (struct((offsets, LANES, channels), BF16), struct((offsets, LANES, wide), BF16)),
        (kernel_one, kernel_two),
        fetch=2,
        scratch=(
            pltpu.VMEM(kernel_one.shape, BF16),
            pltpu.VMEM(kernel_two.shape, BF16),
            pltpu.SemaphoreType.DMA((2,)),
        ),
        cost=pl.CostEstimate(flops=10**8, bytes_accessed=10**7, transcendentals=0),
    )
    first, second, *weights = lax.optimization_barrier((first, second, *weights))
    first_far, second_far = exchanged(first, "split", 1), exchanged(second, "split", 1)

    tile_rows = 3 * -(-offsets // 4) * (outs + channels)
    half = up_to(tile_rows, 4 * regions * 8) // 4
    kept, sent = struct((half, LANES), F32), struct((half, LANES), BF16)
    output, *sums = call(
        main_kernel,
        (struct((outs, voxels), BF16), kept, kept, sent, sent),
        (position, neighbors, packed, partner, first, second, first_far, second_far, turned, *weights),
        scalars=2,
        scratch=(
            pltpu.VMEM((12, 24, 24, LANES), F32),
            pltpu.VMEM((10, 24, 24, wide), F32),
            pltpu.VMEM((10, 10, 24, LANES), F32),
            pltpu.VMEM((4 * half, LANES), F32),
            pltpu.VMEM((3, 2, 12, 96, LANES), BF16),
            pltpu.VMEM((3, 3, 12, 16, LANES), BF16),
            pltpu.VMEM((3, 2, 10, 80, LANES), BF16),
            pltpu.VMEM((3, 2, 10, 80, wide), BF16),
        ),
    )

    sums = [sums[part] + exchanged(sums[2 + part], "split", 1).astype(F32) for part in range(2)]
    bits = list(range((regions - 1).bit_length()))
    orders = [bits, bits[1::-1] + bits[2:]]

    for step in range(len(bits) - 1):
        for part, order in enumerate(orders):
            mask = 1 << order[step]
            keep, give = halves(sums[part], (region // mask) % 2)
            sums[part] = keep + exchanged(give.astype(BF16), "region", mask).astype(F32)
    for part, order in enumerate(orders):
        own = sums[part].astype(BF16)
        sums[part] = (own.astype(F32) + exchanged(own, "region", 1 << order[-1]).astype(F32)).astype(BF16)

    def joined(own, other, bit):
        return jnp.where(bit == 0, jnp.concatenate([own, other], 0), jnp.concatenate([other, own], 0))

    for step in reversed(range(len(bits) - 1)):
        for part, order in enumerate(orders):
            mask = 1 << order[step]
            sums[part] = joined(sums[part], exchanged(sums[part], "region", mask), (region // mask) % 2)
    ends = [value for own in sums for value in (own, exchanged(own, "split", 1))]
    grad_one, grad_two = call(
        unpack_kernel,
        (struct((offsets, channels, channels), F32), struct((offsets, channels, outs), F32)),
        (position, *ends),
        scalars=1,
        scratch=(pltpu.VMEM((4 * half, LANES), BF16),),
    )
    return output, grad_one, grad_two


def solution(mesh):
    rows = P(("region", "split"), None)
    columns = P(None, ("region", "split"))
    return jax.shard_map(
        shards,
        mesh=mesh,
        in_specs=(columns, P(), P(), rows, rows, columns),
        out_specs=(columns, P(), P()),
        check_vma=False,
    )
```

```python
import functools

import jax
import jax.numpy as jnp
from jax import lax
from jax.experimental import pallas as pl
from jax.experimental.pallas import tpu as pltpu
from jax.sharding import PartitionSpec as P

F32 = jnp.float32
BF16 = jnp.bfloat16
LANES = 128
VMEM_BYTES = 32 * 2**20


def up_to(value, step):
    return -(-value // step) * step


def store_planes(target_ref, rows, upper):
    row = pl.multiple_of(upper * 384, 128)
    near = pl.multiple_of(upper * 448, 64)
    target_ref[:, :LANES] = rows[pl.ds(row, 128), :LANES]
    target_ref[:64, LANES:] = rows[pl.ds(near, 64), LANES : 2 * LANES]
    target_ref[64:, LANES:] = rows[pl.ds(near, 64), 2 * LANES :]


def pack_kernel(stack_ref, packed_ref, first_ref, second_ref):
    packed_ref[...] = stack_ref[...].astype(F32).T.astype(BF16)
    odd = lax.axis_index("region") % 2
    store_planes(first_ref, packed_ref, 1 - odd)
    store_planes(second_ref, packed_ref, odd)


def store_turned(total_ref, product, offset, first_row, channels):
    rows = product.shape[0]
    spare = LANES - channels
    group, place = divmod(offset, 4)
    if place < 3:
        base = first_row + (3 * group + place) * rows
        total_ref[pl.ds(base, rows), :channels] = product[:, :channels]
    else:
        for piece in range(3):
            base = first_row + (3 * group + piece) * rows
            total_ref[pl.ds(base, rows), channels:] = product[:, piece * spare : (piece + 1) * spare]


TAPS = range(27)
CHUNKS = [TAPS[first : first + 6] for first in range(0, 27, 6)]


def offset_of(tap):
    return 9 * (tap % 3) + tap // 3


def staged(target, tap, count, more=0):
    code, dx = divmod(tap, 3)
    dy, dz = divmod(code, 3)
    row = 16 * ((dy + more) // 2)
    first = dx + more
    block = target[dz, (dy + more) % 2, first : first + count, row : row + 8 * count, :]
    return block.reshape(8 * count * count, target.shape[4])


def second_layer_kernel(occupancy_ref, hidden_s, two_ref, output_ref):
    outs = output_ref.shape[0]
    output = None
    for chunk in CHUNKS:
        rows = jnp.concatenate([staged(hidden_s, tap, 8) for tap in chunk], 1)
        kernel = jnp.concatenate([two_ref[offset_of(tap)] for tap in chunk], 0)[:, :outs]
        term = jnp.dot(rows, kernel, preferred_element_type=F32)
        output = term if output is None else output + term
    output_ref[...] = jnp.where(occupancy_ref[...] > 0, output.T, 0.0).astype(BF16)


def main_kernel(
    outs, neighbors_ref, own_ref, partner_ref, first_ref, second_ref, first_far_ref, second_far_ref,
    stack_ref, one_ref, two_ref, kept_p_ref, kept_q_ref, sent_p_ref, sent_q_ref, hidden_s,
    masked_w, grad_w, hidden_w, total, masked_s, plane_s, grad_s,
):
    odd, split = lax.axis_index("region") % 2, lax.axis_index("split")
    channels = one_ref.shape[2]
    wide = grad_w.shape[3]
    masked_w[:, 6:18] = jnp.zeros((12, 12, 24, LANES), F32)
    grad_w[:, 7:17] = jnp.zeros((10, 10, 24, wide), F32)

    own = own_ref[...].astype(F32).reshape(8, 8, 8, LANES + wide)
    masked_w[2:10, 8:16, 8:16, :] = own[..., :LANES]
    grad_w[1:9, 8:16, 8:16, :] = own[..., LANES:]

    def placed(step_x, step_z):
        found = [neighbors_ref[0, 9 * (step_x + 1) + 3 * step_y + step_z + 1] >= 0 for step_y in range(3)]
        y = jnp.where(found[0], 0, jnp.where(found[1], 1, 2))
        return found[0] | found[1] | found[2], pl.multiple_of(8 * y, 8)

    step_z = 1 - 2 * split
    valid, y = placed(0, step_z)
    z = pl.multiple_of(8 + 8 * step_z, 8)

    @pl.when(valid)
    def _():
        block = partner_ref[...].astype(F32).reshape(8, 8, 8, LANES + wide)
        masked_w[2:10, pl.ds(y, 8), pl.ds(z, 8), :] = block[..., :LANES]
        grad_w[1:9, pl.ds(y, 8), pl.ds(z, 8), :] = block[..., LANES:]

    for which, refs in enumerate(((first_ref, first_far_ref), (second_ref, second_far_ref))):
        step_x = 1 - 2 * odd if which == 0 else 2 * odd - 1
        for source, ref in enumerate(refs):
            step_z = 0 if source == 0 else 1 - 2 * split
            valid, y = placed(step_x, step_z)
            z = pl.multiple_of(8 + 8 * step_z, 8)
            x_masked = jnp.where(step_x > 0, 10, 0)
            x_grad = jnp.where(step_x > 0, 9, 0)

            @pl.when(valid)
            def _():
                block = ref[...].astype(F32)
                masked_w[pl.ds(x_masked, 2), pl.ds(y, 8), pl.ds(z, 8), :] = block[:, :LANES].reshape(2, 8, 8, LANES)
                near = jnp.concatenate([block[:64, LANES:], block[64:, LANES:]], 1)
                grad_w[pl.ds(x_grad, 1), pl.ds(y, 8), pl.ds(z, 8), :] = near.reshape(1, 8, 8, wide)

    def stage(target, source, first_x, first_y, first_z):
        count_x, rows = target.shape[2:4]
        lanes = target.shape[4]
        for dz in range(3):
            block = source[
                first_x : first_x + count_x, first_y : first_y + rows // 8, first_z + dz : first_z + dz + 8, :
            ]
            target[dz, 0] = block.reshape(count_x, rows, lanes).astype(BF16)
            target[dz, 1, :, : rows - 16] = block[:, 1 : rows // 8 - 1].reshape(count_x, rows - 16, lanes).astype(BF16)

    beside = 16 - 9 * split
    stage(masked_s, masked_w, 0, 6, 7)
    for dz in range(3):
        plane = masked_w[:, 6:24, pl.ds(beside - 1 + dz, 1), :].reshape(12, 18, LANES)
        for dy in range(3):
            plane_s[dz, dy] = plane[:, dy : dy + 16, :].astype(BF16)
        if dz == 1:
            plane_flag = plane[1:11, 1:17, channels : channels + 1].reshape(160, 1) > 0

    def plane_rows(tap):
        code, dx = divmod(tap, 3)
        dy, dz = divmod(code, 3)
        return plane_s[dz, dy, dx : dx + 10].reshape(160, LANES)

    hidden_pre = None
    for chunk in CHUNKS:
        rows = jnp.concatenate(
            [jnp.concatenate([staged(masked_s, tap, 10), plane_rows(tap)], 0) for tap in chunk], 1
        )
        kernel = jnp.concatenate([one_ref[offset_of(tap)] for tap in chunk], 0)
        term = jnp.dot(rows, kernel, preferred_element_type=F32)
        hidden_pre = term if hidden_pre is None else hidden_pre + term
    flags = masked_w[1:11, 7:17, 8:16, channels : channels + 1].reshape(800, 1) > 0
    hidden_pre = jnp.where(jnp.concatenate([flags, plane_flag], 0), hidden_pre, 0.0)
    hidden = hidden_pre * jax.nn.sigmoid(hidden_pre)
    hidden = jnp.concatenate([hidden, jnp.zeros((960, LANES - channels), F32)], 1)
    hidden_w[:, :, 8:16, :] = hidden[:800].reshape(10, 10, 8, LANES)
    hidden_w[:, :, 0:8, :] = jnp.zeros((10, 10, 8, LANES), F32)
    hidden_w[:, :, 16:24, :] = jnp.zeros((10, 10, 8, LANES), F32)
    hidden_w[:, :, pl.ds(beside, 1), :] = hidden[800:].reshape(10, 16, LANES)[:, :10].reshape(10, 10, 1, LANES)
    own_pre = hidden_pre[:800].reshape(10, 10, 8, channels)[1:9, 1:9].reshape(512, channels)
    own_flag = masked_w[2:10, 8:16, 8:16, channels : channels + 1].reshape(512, 1) > 0

    first_one = 3 * (-(-27 // 4)) * outs
    turned_out = stack_ref[LANES : LANES + outs, :]
    stage(hidden_s, hidden_w, 0, 0, 7)
    for chunk in CHUNKS:
        rows = jnp.concatenate([staged(hidden_s, tap, 8) for tap in chunk], 1)
        product = jnp.dot(turned_out, rows, preferred_element_type=F32)
        for place, tap in enumerate(chunk):
            store_turned(total, product[:, place * LANES : (place + 1) * LANES], offset_of(tap), 0, channels)

    stage(grad_s, grad_w, 0, 7, 7)
    back = None
    for chunk in CHUNKS:
        rows = jnp.concatenate([staged(grad_s, tap, 8) for tap in chunk], 1)
        kernel = jnp.concatenate([two_ref[26 - offset_of(tap)] for tap in chunk], 1)
        term = lax.dot_general(rows, kernel, (((1,), (1,)), ((), ())), preferred_element_type=F32)
        back = term if back is None else back + term
    back = back[:, :channels]
    gate = jax.nn.sigmoid(own_pre)
    grad_pre = jnp.where(own_flag, back * gate * (1.0 + own_pre * (1.0 - gate)), 0.0)
    turned_pre = grad_pre.T.astype(BF16)

    for chunk in CHUNKS:
        rows = jnp.concatenate([staged(masked_s, tap, 8, 1) for tap in chunk], 1)
        product = jnp.dot(turned_pre, rows, preferred_element_type=F32)
        for place, tap in enumerate(chunk):
            store_turned(
                total, product[:, place * LANES : (place + 1) * LANES], offset_of(tap), first_one, channels
            )

    half = kept_p_ref.shape[0]
    for start, kept_ref, sent_ref in ((0, kept_p_ref, sent_p_ref), (2 * half, kept_q_ref, sent_q_ref)):
        kept_ref[...] = total[pl.ds(pl.multiple_of(start + split * half, 16), half), :]
        sent_ref[...] = total[pl.ds(pl.multiple_of(start + (1 - split) * half, 16), half), :].astype(BF16)


def unpack_kernel(own_p_ref, other_p_ref, own_q_ref, other_q_ref, one_hbm, two_hbm, sums, one_ref, two_ref, sems):
    split = lax.axis_index("split")
    offsets, channels, outs = two_ref.shape
    half = own_p_ref.shape[0]
    for start, own_ref, other_ref in ((0, own_p_ref, other_p_ref), (2 * half, own_q_ref, other_q_ref)):
        sums[pl.ds(pl.multiple_of(start + split * half, 16), half), :] = own_ref[...]
        sums[pl.ds(pl.multiple_of(start + (1 - split) * half, 16), half), :] = other_ref[...]
    row = lax.broadcasted_iota(jnp.int32, (LANES, LANES), 0)
    unit = jnp.where(row == lax.broadcasted_iota(jnp.int32, (LANES, LANES), 1), 1.0, 0.0).astype(BF16)
    spare = LANES - channels
    fours = -(-offsets // 4)
    copies = []
    for ref, target, first, rows in ((two_ref, two_hbm, 0, outs), (one_ref, one_hbm, 3 * fours * outs, channels)):
        for group in range(fours):
            for place in range(3):
                part = sums[pl.ds(first + (3 * group + place) * rows, rows), :]
                part = lax.dot_general(unit, part, (((1,), (1,)), ((), ())), preferred_element_type=F32)
                ref[4 * group + place] = part[:channels]
                if 4 * group + 3 < offsets:
                    ref[4 * group + 3, place * spare : (place + 1) * spare, :] = part[channels:]
            done = pl.ds(4 * group, min(4, offsets - 4 * group))
            copies.append(pltpu.make_async_copy(ref.at[done], target.at[done], sems.at[len(copies)]))
            copies[-1].start()
    for copy in copies:
        copy.wait()


def call(kernel, out_shape, args, scalars=0, scratch=(), cost=None, into=pltpu.VMEM):
    spaces = [pltpu.SMEM] * scalars + [pltpu.VMEM] * (len(args) - scalars)
    return pl.pallas_call(
        kernel,
        out_shape=out_shape,
        in_specs=[pl.BlockSpec(memory_space=space) for space in spaces],
        out_specs=jax.tree.map(lambda _: pl.BlockSpec(memory_space=into), out_shape),
        scratch_shapes=list(scratch),
        compiler_params=pltpu.CompilerParams(vmem_limit_bytes=VMEM_BYTES),
        cost_estimate=cost,
    )(*args)


def exchanged(value, axis, mask):
    return lax.ppermute(value, axis, [(i, i ^ mask) for i in range(lax.axis_size(axis))])


def halves(value, bit):
    half = value.shape[0] // 2
    return (
        lax.dynamic_slice_in_dim(value, bit * half, half, 0),
        lax.dynamic_slice_in_dim(value, (1 - bit) * half, half, 0),
    )


def shards(features, kernel_one, kernel_two, occupancy, neighbors, cotangent):
    channels, voxels = features.shape
    offsets, _, outs = kernel_two.shape
    regions = lax.axis_size("region")
    region = lax.axis_index("region").astype(jnp.int32)
    split = lax.axis_index("split").astype(jnp.int32)
    wide = up_to(outs, LANES)
    struct = jax.ShapeDtypeStruct

    stack = jnp.concatenate(
        [
            features,
            jnp.ones((LANES - channels, voxels), BF16),
            cotangent,
            jnp.zeros((wide - outs, voxels), BF16),
        ],
        0,
    )
    stack = jnp.where(occupancy > 0, stack, jnp.zeros((), BF16))
    planes = struct((128, 2 * LANES), BF16)
    packed, first, second = call(pack_kernel, (struct((voxels, LANES + wide), BF16), planes, planes), (stack,))
    pairs = [(i, i + 1) for i in range(1, regions - 1, 2)]
    second = lax.ppermute(second, "region", pairs + [(b, a) for a, b in pairs])
    first = lax.ppermute(first, "region", [(i, i ^ 1) for i in range(regions)])
    partner = exchanged(packed, "split", 1)
    one = jnp.pad(kernel_one, ((0, 0), (0, LANES - channels), (0, 0)))
    two = jnp.pad(kernel_two, ((0, 0), (0, LANES - channels), (0, wide - outs)))
    first, second, one, two = lax.optimization_barrier((first, second, one, two))
    first_far, second_far = exchanged(first, "split", 1), exchanged(second, "split", 1)

    tile_rows = 3 * -(-offsets // 4) * (outs + channels)
    half = up_to(tile_rows, 4 * regions * 8) // 4
    kept, sent = struct((half, LANES), F32), struct((half, LANES), BF16)
    *sums, hidden = call(
        functools.partial(main_kernel, outs),
        (kept, kept, sent, sent, struct((3, 2, 10, 80, LANES), BF16)),
        (neighbors, packed, partner, first, second, first_far, second_far, stack, one, two),
        scalars=1,
        scratch=(
            pltpu.VMEM((12, 24, 24, LANES), F32),
            pltpu.VMEM((10, 24, 24, wide), F32),
            pltpu.VMEM((10, 10, 24, LANES), F32),
            pltpu.VMEM((4 * half, LANES), F32),
            pltpu.VMEM((3, 2, 12, 96, LANES), BF16),
            pltpu.VMEM((3, 3, 12, 16, LANES), BF16),
            pltpu.VMEM((3, 2, 10, 80, wide), BF16),
        ),
    )
    sums = [sums[part] + exchanged(sums[2 + part], "split", 1).astype(F32) for part in range(2)]
    sums[0], hidden = lax.optimization_barrier((sums[0], hidden))
    output = call(
        second_layer_kernel,
        struct((outs, voxels), BF16),
        (occupancy, hidden, two),
        cost=pl.CostEstimate(flops=2 * voxels * offsets * channels * outs, bytes_accessed=4 * 2**20, transcendentals=0),
    )
    bits = list(range((regions - 1).bit_length()))
    orders = [bits, bits[1::-1] + bits[2:]]

    for step in range(len(bits) - 1):
        pieces = []
        for part, order in enumerate(orders):
            mask = 1 << order[step]
            keep, give = halves(sums[part], (region // mask) % 2)
            pieces.append((keep, exchanged(give.astype(BF16), "region", mask)))
        if step == 0:
            pieces[0], output = lax.optimization_barrier((pieces[0], output))
        sums = [keep + came.astype(F32) for keep, came in pieces]
    for part, order in enumerate(orders):
        own = sums[part].astype(BF16)
        sums[part] = (own.astype(F32) + exchanged(own, "region", 1 << order[-1]).astype(F32)).astype(BF16)

    def joined(own, other, bit):
        return jnp.where(bit == 0, jnp.concatenate([own, other], 0), jnp.concatenate([other, own], 0))

    for step in reversed(range(len(bits) - 1)):
        for part, order in enumerate(orders):
            mask = 1 << order[step]
            sums[part] = joined(sums[part], exchanged(sums[part], "region", mask), (region // mask) % 2)
    ends = [value for own in sums for value in (own, exchanged(own, "split", 1))]
    grad_one, grad_two = call(
        unpack_kernel,
        (struct((offsets, channels, channels), F32), struct((offsets, channels, outs), F32)),
        ends,
        scratch=(
            pltpu.VMEM((4 * half, LANES), BF16),
            pltpu.VMEM((offsets, channels, channels), F32),
            pltpu.VMEM((offsets, channels, outs), F32),
            pltpu.SemaphoreType.DMA((2 * -(-offsets // 4),)),
        ),
        into=pltpu.HBM,
    )
    return output, grad_one, grad_two


def solution(mesh):
    rows = P(("region", "split"), None)
    columns = P(None, ("region", "split"))
    return jax.shard_map(
        shards,
        mesh=mesh,
        in_specs=(columns, P(), P(), rows, rows, columns),
        out_specs=(columns, P(), P()),
        check_vma=False,
    )
```

```python
import functools

import jax
import jax.numpy as jnp
from jax import lax
from jax.experimental import pallas as pl
from jax.experimental.pallas import tpu as pltpu
from jax.sharding import PartitionSpec as P

F32 = jnp.float32
BF16 = jnp.bfloat16
LANES = 128


def up_to(value, step):
    return -(-value // step) * step


def store_planes(target_ref, rows, upper):
    row = pl.multiple_of(upper * 384, 128)
    near = pl.multiple_of(upper * 448, 64)
    target_ref[:, :LANES] = rows[pl.ds(row, 128), :LANES]
    target_ref[:64, LANES:] = rows[pl.ds(near, 64), LANES : 2 * LANES]
    target_ref[64:, LANES:] = rows[pl.ds(near, 64), 2 * LANES :]


def pack_kernel(channels, stack_ref, occupancy_ref, packed_ref, first_ref, second_ref, turned_ref):
    active = occupancy_ref[...] > 0
    row = lax.broadcasted_iota(jnp.int32, stack_ref.shape, 0)
    masked = jnp.where(active, jnp.where(row == channels, 1.0, stack_ref[...].astype(F32)), 0.0)
    packed_ref[...] = masked.T.astype(BF16)
    turned_ref[...] = masked[LANES : LANES + turned_ref.shape[0]].astype(BF16)
    odd = lax.axis_index("region") % 2
    store_planes(first_ref, packed_ref, 1 - odd)
    store_planes(second_ref, packed_ref, odd)


def store_turned(total_ref, product, offset, first_row, channels):
    rows = product.shape[0]
    spare = LANES - channels
    group, place = divmod(offset, 4)
    if place < 3:
        base = first_row + (3 * group + place) * rows
        total_ref[pl.ds(base, rows), :channels] = product[:, :channels]
    else:
        for piece in range(3):
            base = first_row + (3 * group + piece) * rows
            total_ref[pl.ds(base, rows), channels:] = product[:, piece * spare : (piece + 1) * spare]


TAPS = range(27)
CHUNKS = [TAPS[first : first + 6] for first in range(0, 27, 6)]


def offset_of(tap):
    return 9 * (tap % 3) + tap // 3


def staged(target, tap, count, more=0):
    code, dx = divmod(tap, 3)
    dy, dz = divmod(code, 3)
    row = 16 * ((dy + more) // 2)
    first = dx + more
    block = target[dz, (dy + more) % 2, first : first + count, row : row + 8 * count, :]
    return block.reshape(8 * count * count, target.shape[4])


def main_kernel(
    neighbors_ref, own_ref, partner_ref, first_ref, second_ref, first_far_ref, second_far_ref,
    turned_ref, one_ref, two_ref, output_ref, kept_p_ref, kept_q_ref, sent_p_ref, sent_q_ref,
    masked_w, grad_w, hidden_w, total, masked_s, plane_s, hidden_s, grad_s,
):
    odd, split = lax.axis_index("region") % 2, lax.axis_index("split")
    channels = one_ref.shape[2]
    wide = grad_w.shape[3]
    outs = turned_ref.shape[0]
    masked_w[:, 6:18] = jnp.zeros((12, 12, 24, LANES), F32)
    grad_w[:, 7:17] = jnp.zeros((10, 10, 24, wide), F32)

    own = own_ref[...].astype(F32).reshape(8, 8, 8, LANES + wide)
    masked_w[2:10, 8:16, 8:16, :] = own[..., :LANES]
    grad_w[1:9, 8:16, 8:16, :] = own[..., LANES:]

    def placed(step_x, step_z):
        found = [neighbors_ref[0, 9 * (step_x + 1) + 3 * step_y + step_z + 1] >= 0 for step_y in range(3)]
        y = jnp.where(found[0], 0, jnp.where(found[1], 1, 2))
        return found[0] | found[1] | found[2], pl.multiple_of(8 * y, 8)

    step_z = 1 - 2 * split
    valid, y = placed(0, step_z)
    z = pl.multiple_of(8 + 8 * step_z, 8)

    @pl.when(valid)
    def _():
        block = partner_ref[...].astype(F32).reshape(8, 8, 8, LANES + wide)
        masked_w[2:10, pl.ds(y, 8), pl.ds(z, 8), :] = block[..., :LANES]
        grad_w[1:9, pl.ds(y, 8), pl.ds(z, 8), :] = block[..., LANES:]

    for which, refs in enumerate(((first_ref, first_far_ref), (second_ref, second_far_ref))):
        step_x = 1 - 2 * odd if which == 0 else 2 * odd - 1
        for source, ref in enumerate(refs):
            step_z = 0 if source == 0 else 1 - 2 * split
            valid, y = placed(step_x, step_z)
            z = pl.multiple_of(8 + 8 * step_z, 8)
            x_masked = jnp.where(step_x > 0, 10, 0)
            x_grad = jnp.where(step_x > 0, 9, 0)

            @pl.when(valid)
            def _():
                block = ref[...].astype(F32)
                masked_w[pl.ds(x_masked, 2), pl.ds(y, 8), pl.ds(z, 8), :] = block[:, :LANES].reshape(2, 8, 8, LANES)
                near = jnp.concatenate([block[:64, LANES:], block[64:, LANES:]], 1)
                grad_w[pl.ds(x_grad, 1), pl.ds(y, 8), pl.ds(z, 8), :] = near.reshape(1, 8, 8, wide)

    def stage(target, source, first_x, first_y, first_z):
        count_x, rows = target.shape[2:4]
        lanes = target.shape[4]
        for dz in range(3):
            block = source[
                first_x : first_x + count_x, first_y : first_y + rows // 8, first_z + dz : first_z + dz + 8, :
            ]
            target[dz, 0] = block.reshape(count_x, rows, lanes).astype(BF16)
            target[dz, 1, :, : rows - 16] = block[:, 1 : rows // 8 - 1].reshape(count_x, rows - 16, lanes).astype(BF16)

    beside = 16 - 9 * split
    stage(masked_s, masked_w, 0, 6, 7)
    for dz in range(3):
        plane = masked_w[:, 6:24, pl.ds(beside - 1 + dz, 1), :].reshape(12, 18, LANES)
        for dy in range(3):
            plane_s[dz, dy] = plane[:, dy : dy + 16, :].astype(BF16)
        if dz == 1:
            plane_flag = plane[1:11, 1:17, channels : channels + 1].reshape(160, 1) > 0

    def plane_rows(tap):
        code, dx = divmod(tap, 3)
        dy, dz = divmod(code, 3)
        return plane_s[dz, dy, dx : dx + 10].reshape(160, LANES)

    hidden_pre = None
    for chunk in CHUNKS:
        rows = jnp.concatenate(
            [jnp.concatenate([staged(masked_s, tap, 10), plane_rows(tap)], 0) for tap in chunk], 1
        )
        kernel = jnp.concatenate([one_ref[offset_of(tap)] for tap in chunk], 0)
        term = jnp.dot(rows, kernel, preferred_element_type=F32)
        hidden_pre = term if hidden_pre is None else hidden_pre + term
    flags = masked_w[1:11, 7:17, 8:16, channels : channels + 1].reshape(800, 1) > 0
    hidden_pre = jnp.where(jnp.concatenate([flags, plane_flag], 0), hidden_pre, 0.0)
    hidden = hidden_pre * jax.nn.sigmoid(hidden_pre)
    hidden = jnp.concatenate([hidden, jnp.zeros((960, LANES - channels), F32)], 1)
    hidden_w[:, :, 8:16, :] = hidden[:800].reshape(10, 10, 8, LANES)
    hidden_w[:, :, 0:8, :] = jnp.zeros((10, 10, 8, LANES), F32)
    hidden_w[:, :, 16:24, :] = jnp.zeros((10, 10, 8, LANES), F32)
    hidden_w[:, :, pl.ds(beside, 1), :] = hidden[800:].reshape(10, 16, LANES)[:, :10].reshape(10, 10, 1, LANES)
    own_pre = hidden_pre[:800].reshape(10, 10, 8, channels)[1:9, 1:9].reshape(512, channels)
    own_flag = masked_w[2:10, 8:16, 8:16, channels : channels + 1].reshape(512, 1) > 0

    first_one = 3 * (-(-27 // 4)) * outs
    turned_out = turned_ref[...]
    stage(hidden_s, hidden_w, 0, 0, 7)
    output = None
    for chunk in CHUNKS:
        rows = jnp.concatenate([staged(hidden_s, tap, 8) for tap in chunk], 1)
        kernel = jnp.concatenate([two_ref[offset_of(tap)] for tap in chunk], 0)[:, :outs]
        term = jnp.dot(rows, kernel, preferred_element_type=F32)
        output = term if output is None else output + term
        product = jnp.dot(turned_out, rows, preferred_element_type=F32)
        for place, tap in enumerate(chunk):
            store_turned(total, product[:, place * LANES : (place + 1) * LANES], offset_of(tap), 0, channels)

    output_ref[...] = jnp.where(own_flag, output, 0.0).T.astype(BF16)

    stage(grad_s, grad_w, 0, 7, 7)
    back = None
    for chunk in CHUNKS:
        rows = jnp.concatenate([staged(grad_s, tap, 8) for tap in chunk], 1)
        kernel = jnp.concatenate([two_ref[26 - offset_of(tap)] for tap in chunk], 1)
        term = lax.dot_general(rows, kernel, (((1,), (1,)), ((), ())), preferred_element_type=F32)
        back = term if back is None else back + term
    back = back[:, :channels]
    gate = jax.nn.sigmoid(own_pre)
    grad_pre = jnp.where(own_flag, back * gate * (1.0 + own_pre * (1.0 - gate)), 0.0)
    turned_pre = grad_pre.T.astype(BF16)

    for chunk in CHUNKS:
        rows = jnp.concatenate([staged(masked_s, tap, 8, 1) for tap in chunk], 1)
        product = jnp.dot(turned_pre, rows, preferred_element_type=F32)
        for place, tap in enumerate(chunk):
            store_turned(
                total, product[:, place * LANES : (place + 1) * LANES], offset_of(tap), first_one, channels
            )

    half = kept_p_ref.shape[0]
    for start, kept_ref, sent_ref in ((0, kept_p_ref, sent_p_ref), (2 * half, kept_q_ref, sent_q_ref)):
        kept_ref[...] = total[pl.ds(pl.multiple_of(start + split * half, 16), half), :]
        sent_ref[...] = total[pl.ds(pl.multiple_of(start + (1 - split) * half, 16), half), :].astype(BF16)


def unpack_kernel(own_p_ref, other_p_ref, own_q_ref, other_q_ref, one_hbm, two_hbm, sums, one_ref, two_ref, sems):
    split = lax.axis_index("split")
    offsets, channels, outs = two_ref.shape
    half = own_p_ref.shape[0]
    for start, own_ref, other_ref in ((0, own_p_ref, other_p_ref), (2 * half, own_q_ref, other_q_ref)):
        sums[pl.ds(pl.multiple_of(start + split * half, 16), half), :] = own_ref[...]
        sums[pl.ds(pl.multiple_of(start + (1 - split) * half, 16), half), :] = other_ref[...]
    row = lax.broadcasted_iota(jnp.int32, (LANES, LANES), 0)
    unit = jnp.where(row == lax.broadcasted_iota(jnp.int32, (LANES, LANES), 1), 1.0, 0.0).astype(BF16)
    spare = LANES - channels
    fours = -(-offsets // 4)
    copies = []
    for ref, target, first, rows in ((two_ref, two_hbm, 0, outs), (one_ref, one_hbm, 3 * fours * outs, channels)):
        for group in range(fours):
            for place in range(3):
                part = sums[pl.ds(first + (3 * group + place) * rows, rows), :]
                part = lax.dot_general(unit, part, (((1,), (1,)), ((), ())), preferred_element_type=F32)
                ref[4 * group + place] = part[:channels]
                if 4 * group + 3 < offsets:
                    ref[4 * group + 3, place * spare : (place + 1) * spare, :] = part[channels:]
            done = pl.ds(4 * group, min(4, offsets - 4 * group))
            copies.append(pltpu.make_async_copy(ref.at[done], target.at[done], sems.at[len(copies)]))
            copies[-1].start()
    for copy in copies:
        copy.wait()


def call(kernel, out_shape, args, scalars=0, scratch=(), cost=None, into=pltpu.VMEM, mib=12):
    spaces = [pltpu.SMEM] * scalars + [pltpu.VMEM] * (len(args) - scalars)
    return pl.pallas_call(
        kernel,
        out_shape=out_shape,
        in_specs=[pl.BlockSpec(memory_space=space) for space in spaces],
        out_specs=jax.tree.map(lambda _: pl.BlockSpec(memory_space=into), out_shape),
        scratch_shapes=list(scratch),
        compiler_params=pltpu.CompilerParams(vmem_limit_bytes=mib * 2**20),
        cost_estimate=cost,
    )(*args)


def exchanged(value, axis, mask):
    return lax.ppermute(value, axis, [(i, i ^ mask) for i in range(lax.axis_size(axis))])


def halves(value, bit):
    half = value.shape[0] // 2
    return (
        lax.dynamic_slice_in_dim(value, bit * half, half, 0),
        lax.dynamic_slice_in_dim(value, (1 - bit) * half, half, 0),
    )


def shards(features, kernel_one, kernel_two, occupancy, neighbors, cotangent):
    channels, voxels = features.shape
    offsets, _, outs = kernel_two.shape
    regions = lax.axis_size("region")
    region = lax.axis_index("region").astype(jnp.int32)
    split = lax.axis_index("split").astype(jnp.int32)
    wide = up_to(outs, LANES)
    struct = jax.ShapeDtypeStruct

    spare = LANES - channels
    stack = jnp.pad(features, ((0, spare + wide), (0, 0))) + jnp.pad(cotangent, ((LANES, wide - outs), (0, 0)))
    planes = struct((128, 2 * LANES), BF16)
    packed, first, second, turned = call(
        functools.partial(pack_kernel, channels),
        (struct((voxels, LANES + wide), BF16), planes, planes, struct((outs, voxels), BF16)),
        (stack, occupancy),
    )
    pairs = [(i, i + 1) for i in range(1, regions - 1, 2)]
    second = lax.ppermute(second, "region", pairs + [(b, a) for a, b in pairs])
    first = lax.ppermute(first, "region", [(i, i ^ 1) for i in range(regions)])
    partner = exchanged(packed, "split", 1)
    one = jnp.pad(kernel_one, ((0, 0), (0, LANES - channels), (0, 0)))
    two = jnp.pad(kernel_two, ((0, 0), (0, LANES - channels), (0, wide - outs)))
    second, one, two = lax.optimization_barrier((second, one, two))
    second_far = exchanged(second, "split", 1)
    first_far = exchanged(first, "split", 1)

    tile_rows = 3 * -(-offsets // 4) * (outs + channels)
    half = up_to(tile_rows, 4 * regions * 8) // 4
    kept, sent = struct((half, LANES), F32), struct((half, LANES), BF16)
    output, *sums = call(
        main_kernel,
        (struct((outs, voxels), BF16), kept, kept, sent, sent),
        (neighbors, packed, partner, first, second, first_far, second_far, turned, one, two),
        scalars=1,
        mib=26,
        scratch=(
            pltpu.VMEM((12, 24, 24, LANES), F32),
            pltpu.VMEM((10, 24, 24, wide), F32),
            pltpu.VMEM((10, 10, 24, LANES), F32),
            pltpu.VMEM((4 * half, LANES), F32),
            pltpu.VMEM((3, 2, 12, 96, LANES), BF16),
            pltpu.VMEM((3, 3, 12, 16, LANES), BF16),
            pltpu.VMEM((3, 2, 10, 80, LANES), BF16),
            pltpu.VMEM((3, 2, 10, 80, wide), BF16),
        ),
    )
    sums = [sums[part] + exchanged(sums[2 + part], "split", 1).astype(F32) for part in range(2)]
    bits = list(range((regions - 1).bit_length()))
    orders = [bits, bits[1::-1] + bits[2:]]

    for step in range(len(bits) - 1):
        pieces = []
        for part, order in enumerate(orders):
            mask = 1 << order[step]
            keep, give = halves(sums[part], (region // mask) % 2)
            pieces.append((keep, exchanged(give.astype(BF16), "region", mask)))
        sums = [keep + came.astype(F32) for keep, came in pieces]
    for part, order in enumerate(orders):
        own = sums[part].astype(BF16)
        sums[part] = (own.astype(F32) + exchanged(own, "region", 1 << order[-1]).astype(F32)).astype(BF16)

    def joined(own, other, bit):
        return jnp.where(bit == 0, jnp.concatenate([own, other], 0), jnp.concatenate([other, own], 0))

    for step in reversed(range(len(bits) - 1)):
        for part, order in enumerate(orders):
            mask = 1 << order[step]
            sums[part] = joined(sums[part], exchanged(sums[part], "region", mask), (region // mask) % 2)
    ends = [value for own in sums for value in (own, exchanged(own, "split", 1))]
    grad_one, grad_two = call(
        unpack_kernel,
        (struct((offsets, channels, channels), F32), struct((offsets, channels, outs), F32)),
        ends,
        scratch=(
            pltpu.VMEM((4 * half, LANES), BF16),
            pltpu.VMEM((offsets, channels, channels), F32),
            pltpu.VMEM((offsets, channels, outs), F32),
            pltpu.SemaphoreType.DMA((2 * -(-offsets // 4),)),
        ),
        into=pltpu.HBM,
    )
    return output, grad_one, grad_two


def solution(mesh):
    rows = P(("region", "split"), None)
    columns = P(None, ("region", "split"))
    return jax.shard_map(
        shards,
        mesh=mesh,
        in_specs=(columns, P(), P(), rows, rows, columns),
        out_specs=(columns, P(), P()),
        check_vma=False,
    )
```

```python
import functools

import jax
import jax.numpy as jnp
from jax import lax
from jax.experimental import pallas as pl
from jax.experimental.pallas import tpu as pltpu
from jax.sharding import PartitionSpec as P

F32 = jnp.float32
BF16 = jnp.bfloat16
LANES = 128


def up_to(value, step):
    return -(-value // step) * step


def store_planes(target_ref, rows, upper):
    row = pl.multiple_of(upper * 384, 128)
    near = pl.multiple_of(upper * 448, 64)
    target_ref[:, :LANES] = rows[pl.ds(row, 128), :LANES]
    target_ref[:64, LANES:] = rows[pl.ds(near, 64), LANES : 2 * LANES]
    target_ref[64:, LANES:] = rows[pl.ds(near, 64), 2 * LANES :]


def pack_kernel(channels, stack_ref, occupancy_ref, packed_ref, first_ref, second_ref, turned_ref):
    active = occupancy_ref[...] > 0
    row = lax.broadcasted_iota(jnp.int32, stack_ref.shape, 0)
    masked = jnp.where(active, jnp.where(row == channels, 1.0, stack_ref[...].astype(F32)), 0.0)
    packed_ref[...] = masked.T.astype(BF16)
    turned_ref[...] = masked[LANES : LANES + turned_ref.shape[0]].astype(BF16)
    odd = lax.axis_index("region") % 2
    store_planes(first_ref, packed_ref, 1 - odd)
    store_planes(second_ref, packed_ref, odd)


def store_turned(total_ref, product, offset, first_row, channels):
    rows = product.shape[0]
    spare = LANES - channels
    group, place = divmod(offset, 4)
    if place < 3:
        base = first_row + (3 * group + place) * rows
        total_ref[pl.ds(base, rows), :channels] = product[:, :channels]
    else:
        for piece in range(3):
            base = first_row + (3 * group + piece) * rows
            total_ref[pl.ds(base, rows), channels:] = product[:, piece * spare : (piece + 1) * spare]


TAPS = range(27)
CHUNKS = [TAPS[first : first + 6] for first in range(0, 27, 6)]


def offset_of(tap):
    return 9 * (tap % 3) + tap // 3


def staged(target, tap, count, more=0):
    code, dx = divmod(tap, 3)
    dy, dz = divmod(code, 3)
    row = 16 * ((dy + more) // 2)
    first = dx + more
    block = target[dz, (dy + more) % 2, first : first + count, row : row + 8 * count, :]
    return block.reshape(8 * count * count, target.shape[4])


def main_kernel(
    neighbors_ref, own_ref, partner_ref, first_ref, second_ref, first_far_ref, second_far_ref,
    turned_ref, one_ref, two_ref, output_ref, kept_p_ref, kept_q_ref, sent_p_ref, sent_q_ref,
    masked_w, grad_w, hidden_w, total, masked_s, plane_s, hidden_s, grad_s,
):
    odd, split = lax.axis_index("region") % 2, lax.axis_index("split")
    channels = one_ref.shape[2]
    wide = grad_w.shape[3]
    outs = turned_ref.shape[0]
    masked_w[:, 6:18] = jnp.zeros((12, 12, 24, LANES), F32)
    grad_w[:, 7:17] = jnp.zeros((10, 10, 24, wide), F32)

    own = own_ref[...].astype(F32).reshape(8, 8, 8, LANES + wide)
    masked_w[2:10, 8:16, 8:16, :] = own[..., :LANES]
    grad_w[1:9, 8:16, 8:16, :] = own[..., LANES:]

    def placed(step_x, step_z):
        found = [neighbors_ref[0, 9 * (step_x + 1) + 3 * step_y + step_z + 1] >= 0 for step_y in range(3)]
        y = jnp.where(found[0], 0, jnp.where(found[1], 1, 2))
        return found[0] | found[1] | found[2], pl.multiple_of(8 * y, 8)

    step_z = 1 - 2 * split
    valid, y = placed(0, step_z)
    z = pl.multiple_of(8 + 8 * step_z, 8)

    @pl.when(valid)
    def _():
        block = partner_ref[...].astype(F32).reshape(8, 8, 8, LANES + wide)
        masked_w[2:10, pl.ds(y, 8), pl.ds(z, 8), :] = block[..., :LANES]
        grad_w[1:9, pl.ds(y, 8), pl.ds(z, 8), :] = block[..., LANES:]

    for which, refs in enumerate(((first_ref, first_far_ref), (second_ref, second_far_ref))):
        step_x = 1 - 2 * odd if which == 0 else 2 * odd - 1
        for source, ref in enumerate(refs):
            step_z = 0 if source == 0 else 1 - 2 * split
            valid, y = placed(step_x, step_z)
            z = pl.multiple_of(8 + 8 * step_z, 8)
            x_masked = jnp.where(step_x > 0, 10, 0)
            x_grad = jnp.where(step_x > 0, 9, 0)

            @pl.when(valid)
            def _():
                block = ref[...].astype(F32)
                masked_w[pl.ds(x_masked, 2), pl.ds(y, 8), pl.ds(z, 8), :] = block[:, :LANES].reshape(2, 8, 8, LANES)
                near = jnp.concatenate([block[:64, LANES:], block[64:, LANES:]], 1)
                grad_w[pl.ds(x_grad, 1), pl.ds(y, 8), pl.ds(z, 8), :] = near.reshape(1, 8, 8, wide)

    def stage(target, source, first_x, first_y, first_z):
        count_x, rows = target.shape[2:4]
        lanes = target.shape[4]
        for dz in range(3):
            block = source[
                first_x : first_x + count_x, first_y : first_y + rows // 8, first_z + dz : first_z + dz + 8, :
            ]
            target[dz, 0] = block.reshape(count_x, rows, lanes).astype(BF16)
            target[dz, 1, :, : rows - 16] = block[:, 1 : rows // 8 - 1].reshape(count_x, rows - 16, lanes).astype(BF16)

    beside = 16 - 9 * split
    stage(masked_s, masked_w, 0, 6, 7)
    for dz in range(3):
        plane = masked_w[:, 6:24, pl.ds(beside - 1 + dz, 1), :].reshape(12, 18, LANES)
        for dy in range(3):
            plane_s[dz, dy] = plane[:, dy : dy + 16, :].astype(BF16)
        if dz == 1:
            plane_flag = plane[1:11, 1:17, channels : channels + 1].reshape(160, 1) > 0

    def plane_rows(tap):
        code, dx = divmod(tap, 3)
        dy, dz = divmod(code, 3)
        return plane_s[dz, dy, dx : dx + 10].reshape(160, LANES)

    hidden_pre = None
    for chunk in CHUNKS:
        rows = jnp.concatenate(
            [jnp.concatenate([staged(masked_s, tap, 10), plane_rows(tap)], 0) for tap in chunk], 1
        )
        kernel = jnp.concatenate([one_ref[offset_of(tap)] for tap in chunk], 0)
        term = jnp.dot(rows, kernel, preferred_element_type=F32)
        hidden_pre = term if hidden_pre is None else hidden_pre + term
    flags = masked_w[1:11, 7:17, 8:16, channels : channels + 1].reshape(800, 1) > 0
    hidden_pre = jnp.where(jnp.concatenate([flags, plane_flag], 0), hidden_pre, 0.0)
    hidden = hidden_pre * jax.nn.sigmoid(hidden_pre)
    hidden = jnp.concatenate([hidden, jnp.zeros((960, LANES - channels), F32)], 1)
    hidden_w[:, :, 8:16, :] = hidden[:800].reshape(10, 10, 8, LANES)
    hidden_w[:, :, 0:8, :] = jnp.zeros((10, 10, 8, LANES), F32)
    hidden_w[:, :, 16:24, :] = jnp.zeros((10, 10, 8, LANES), F32)
    hidden_w[:, :, pl.ds(beside, 1), :] = hidden[800:].reshape(10, 16, LANES)[:, :10].reshape(10, 10, 1, LANES)
    own_pre = hidden_pre[:800].reshape(10, 10, 8, channels)[1:9, 1:9].reshape(512, channels)
    own_flag = masked_w[2:10, 8:16, 8:16, channels : channels + 1].reshape(512, 1) > 0

    first_one = 3 * (-(-27 // 4)) * outs
    turned_out = turned_ref[...]
    stage(hidden_s, hidden_w, 0, 0, 7)
    output = None
    for chunk in CHUNKS:
        rows = jnp.concatenate([staged(hidden_s, tap, 8) for tap in chunk], 1)
        kernel = jnp.concatenate([two_ref[offset_of(tap)] for tap in chunk], 0)[:, :outs]
        term = jnp.dot(rows, kernel, preferred_element_type=F32)
        output = term if output is None else output + term
        product = jnp.dot(turned_out, rows, preferred_element_type=F32)
        for place, tap in enumerate(chunk):
            store_turned(total, product[:, place * LANES : (place + 1) * LANES], offset_of(tap), 0, channels)

    output_ref[...] = jnp.where(own_flag, output, 0.0).T.astype(BF16)

    stage(grad_s, grad_w, 0, 7, 7)
    back = None
    for chunk in CHUNKS:
        rows = jnp.concatenate([staged(grad_s, tap, 8) for tap in chunk], 1)
        kernel = jnp.concatenate([two_ref[26 - offset_of(tap)] for tap in chunk], 1)
        term = lax.dot_general(rows, kernel, (((1,), (1,)), ((), ())), preferred_element_type=F32)
        back = term if back is None else back + term
    back = back[:, :channels]
    gate = jax.nn.sigmoid(own_pre)
    grad_pre = jnp.where(own_flag, back * gate * (1.0 + own_pre * (1.0 - gate)), 0.0)
    turned_pre = grad_pre.T.astype(BF16)

    for chunk in CHUNKS:
        rows = jnp.concatenate([staged(masked_s, tap, 8, 1) for tap in chunk], 1)
        product = jnp.dot(turned_pre, rows, preferred_element_type=F32)
        for place, tap in enumerate(chunk):
            store_turned(
                total, product[:, place * LANES : (place + 1) * LANES], offset_of(tap), first_one, channels
            )

    half = kept_p_ref.shape[0]
    for start, kept_ref, sent_ref in ((0, kept_p_ref, sent_p_ref), (2 * half, kept_q_ref, sent_q_ref)):
        kept_ref[...] = total[pl.ds(pl.multiple_of(start + split * half, 16), half), :]
        sent_ref[...] = total[pl.ds(pl.multiple_of(start + (1 - split) * half, 16), half), :].astype(BF16)


def assemble(sums, start, own_ref, other_ref):
    split = lax.axis_index("split")
    half = own_ref.shape[0]
    sums[pl.ds(pl.multiple_of(start + split * half, 16), half), :] = own_ref[...]
    sums[pl.ds(pl.multiple_of(start + (1 - split) * half, 16), half), :] = other_ref[...]


def unpack(sums, first, groups, ref, target, sems):
    offsets, channels, outs = ref.shape
    row = lax.broadcasted_iota(jnp.int32, (LANES, LANES), 0)
    unit = jnp.where(row == lax.broadcasted_iota(jnp.int32, (LANES, LANES), 1), 1.0, 0.0).astype(BF16)
    spare = LANES - channels
    copies = []
    for group in groups:
        for place in range(3):
            part = sums[pl.ds(first + (3 * group + place) * outs, outs), :]
            part = lax.dot_general(unit, part, (((1,), (1,)), ((), ())), preferred_element_type=F32)
            ref[4 * group + place] = part[:channels]
            if 4 * group + 3 < offsets:
                ref[4 * group + 3, place * spare : (place + 1) * spare, :] = part[channels:]
        done = pl.ds(4 * group, min(4, offsets - 4 * group))
        copies.append(pltpu.make_async_copy(ref.at[done], target.at[done], sems.at[len(copies)]))
        copies[-1].start()
    return copies


def first_unpack_kernel(groups, own_ref, other_ref, two_hbm, sums, two_ref, sems):
    assemble(sums, 0, own_ref, other_ref)
    for copy in unpack(sums, 0, groups, two_ref, two_hbm, sems):
        copy.wait()


def second_unpack_kernel(
    groups, own_p_ref, other_p_ref, own_q_ref, other_q_ref, _, one_hbm, two_hbm, sums, one_ref, two_ref, one_sems, two_sems
):
    offsets, _, outs = two_ref.shape
    assemble(sums, 0, own_p_ref, other_p_ref)
    assemble(sums, 2 * own_p_ref.shape[0], own_q_ref, other_q_ref)
    fours = -(-offsets // 4)
    copies = unpack(sums, 0, groups, two_ref, two_hbm, two_sems)
    copies += unpack(sums, 3 * fours * outs, range(fours), one_ref, one_hbm, one_sems)
    for copy in copies:
        copy.wait()


def call(kernel, out_shape, args, scalars=0, scratch=(), cost=None, into=pltpu.VMEM, mib=12, filled=False):
    spaces = [pltpu.SMEM] * scalars + [pltpu.VMEM] * (len(args) - scalars)
    if filled:
        spaces[-1] = into
    return pl.pallas_call(
        kernel,
        out_shape=out_shape,
        in_specs=[pl.BlockSpec(memory_space=space) for space in spaces],
        out_specs=jax.tree.map(lambda _: pl.BlockSpec(memory_space=into), out_shape),
        scratch_shapes=list(scratch),
        compiler_params=pltpu.CompilerParams(vmem_limit_bytes=mib * 2**20),
        cost_estimate=cost,
        input_output_aliases={len(args) - 1: len(out_shape) - 1} if filled else {},
    )(*args)


def exchanged(value, axis, mask):
    return lax.ppermute(value, axis, [(i, i ^ mask) for i in range(lax.axis_size(axis))])


def halves(value, bit):
    half = value.shape[0] // 2
    return (
        lax.dynamic_slice_in_dim(value, bit * half, half, 0),
        lax.dynamic_slice_in_dim(value, (1 - bit) * half, half, 0),
    )


def shards(features, kernel_one, kernel_two, occupancy, neighbors, cotangent):
    channels, voxels = features.shape
    offsets, _, outs = kernel_two.shape
    regions = lax.axis_size("region")
    region = lax.axis_index("region").astype(jnp.int32)
    split = lax.axis_index("split").astype(jnp.int32)
    wide = up_to(outs, LANES)
    struct = jax.ShapeDtypeStruct

    spare = LANES - channels
    stack = jnp.pad(features, ((0, spare + wide), (0, 0))) + jnp.pad(cotangent, ((LANES, wide - outs), (0, 0)))
    planes = struct((128, 2 * LANES), BF16)
    packed, first, second, turned = call(
        functools.partial(pack_kernel, channels),
        (struct((voxels, LANES + wide), BF16), planes, planes, struct((outs, voxels), BF16)),
        (stack, occupancy),
    )
    pairs = [(i, i + 1) for i in range(1, regions - 1, 2)]
    second = lax.ppermute(second, "region", pairs + [(b, a) for a, b in pairs])
    first = lax.ppermute(first, "region", [(i, i ^ 1) for i in range(regions)])
    partner = exchanged(packed, "split", 1)
    one = jnp.pad(kernel_one, ((0, 0), (0, LANES - channels), (0, 0)))
    two = jnp.pad(kernel_two, ((0, 0), (0, LANES - channels), (0, wide - outs)))
    second, one, two = lax.optimization_barrier((second, one, two))
    second_far = exchanged(second, "split", 1)
    first_far = exchanged(first, "split", 1)

    tile_rows = 3 * -(-offsets // 4) * (outs + channels)
    half = up_to(tile_rows, 4 * regions * 8) // 4
    kept, sent = struct((half, LANES), F32), struct((half, LANES), BF16)
    output, *sums = call(
        main_kernel,
        (struct((outs, voxels), BF16), kept, kept, sent, sent),
        (neighbors, packed, partner, first, second, first_far, second_far, turned, one, two),
        scalars=1,
        mib=26,
        scratch=(
            pltpu.VMEM((12, 24, 24, LANES), F32),
            pltpu.VMEM((10, 24, 24, wide), F32),
            pltpu.VMEM((10, 10, 24, LANES), F32),
            pltpu.VMEM((4 * half, LANES), F32),
            pltpu.VMEM((3, 2, 12, 96, LANES), BF16),
            pltpu.VMEM((3, 3, 12, 16, LANES), BF16),
            pltpu.VMEM((3, 2, 10, 80, LANES), BF16),
            pltpu.VMEM((3, 2, 10, 80, wide), BF16),
        ),
    )
    sums = [sums[part] + exchanged(sums[2 + part], "split", 1).astype(F32) for part in range(2)]
    bits = list(range((regions - 1).bit_length()))
    orders = [bits[:-2] + bits[:-3:-1], bits[1::-1] + bits[2:]]
    whole_steps = 2

    for step in range(len(bits) - whole_steps):
        for part, order in enumerate(orders):
            mask = 1 << order[step]
            keep, give = halves(sums[part], (region // mask) % 2)
            sums[part] = keep + exchanged(give.astype(BF16), "region", mask).astype(F32)
    for step in range(len(bits) - whole_steps, len(bits)):
        for part, order in enumerate(orders):
            own = sums[part].astype(BF16)
            sums[part] = own.astype(F32) + exchanged(own, "region", 1 << order[step]).astype(F32)
    sums = [value.astype(BF16) for value in sums]

    def joined(own, other, bit):
        return jnp.where(bit == 0, jnp.concatenate([own, other], 0), jnp.concatenate([other, own], 0))

    for step in reversed(range(len(bits) - whole_steps)):
        for part, order in enumerate(orders):
            mask = 1 << order[step]
            sums[part] = joined(sums[part], exchanged(sums[part], "region", mask), (region // mask) % 2)
    ends = [(own, exchanged(own, "split", 1)) for own in sums]
    fours = -(-offsets // 4)
    early = min(fours, 2 * half // (3 * outs))
    one_shape, two_shape = struct((offsets, channels, channels), F32), struct((offsets, channels, outs), F32)
    grad_two = call(
        functools.partial(first_unpack_kernel, range(early)),
        two_shape,
        ends[0],
        scratch=(
            pltpu.VMEM((2 * half, LANES), BF16),
            pltpu.VMEM(two_shape.shape, F32),
            pltpu.SemaphoreType.DMA((fours,)),
        ),
        cost=pl.CostEstimate(flops=10**8, bytes_accessed=4 * 2**20, transcendentals=0),
        into=pltpu.HBM,
    )
    grad_one, grad_two = call(
        functools.partial(second_unpack_kernel, range(early, fours)),
        (one_shape, two_shape),
        (*ends[0], *ends[1], grad_two),
        scratch=(
            pltpu.VMEM((4 * half, LANES), BF16),
            pltpu.VMEM(one_shape.shape, F32),
            pltpu.VMEM(two_shape.shape, F32),
            pltpu.SemaphoreType.DMA((fours,)),
            pltpu.SemaphoreType.DMA((fours,)),
        ),
        into=pltpu.HBM,
        filled=True,
    )
    return output, grad_one, grad_two


def solution(mesh):
    rows = P(("region", "split"), None)
    columns = P(None, ("region", "split"))
    return jax.shard_map(
        shards,
        mesh=mesh,
        in_specs=(columns, P(), P(), rows, rows, columns),
        out_specs=(columns, P(), P()),
        check_vma=False,
    )
```

```python
import functools

import jax
import jax.numpy as jnp
from jax import lax
from jax.experimental import pallas as pl
from jax.experimental.pallas import tpu as pltpu
from jax.sharding import PartitionSpec as P

F32 = jnp.float32
BF16 = jnp.bfloat16
LANES = 128


def up_to(value, step):
    return -(-value // step) * step


def store_planes(target_ref, rows, upper):
    row = pl.multiple_of(upper * 384, 128)
    near = pl.multiple_of(upper * 448, 64)
    target_ref[:, :LANES] = rows[pl.ds(row, 128), :LANES]
    target_ref[:64, LANES:] = rows[pl.ds(near, 64), LANES : 2 * LANES]
    target_ref[64:, LANES:] = rows[pl.ds(near, 64), 2 * LANES :]


def pack_kernel(channels, stack_ref, occupancy_ref, packed_ref, first_ref, second_ref, turned_ref):
    active = occupancy_ref[...] > 0
    row = lax.broadcasted_iota(jnp.int32, stack_ref.shape, 0)
    masked = jnp.where(active, jnp.where(row == channels, 1.0, stack_ref[...].astype(F32)), 0.0)
    packed_ref[...] = masked.T.astype(BF16)
    turned_ref[...] = masked[LANES : LANES + turned_ref.shape[0]].astype(BF16)
    odd = lax.axis_index("region") % 2
    store_planes(first_ref, packed_ref, 1 - odd)
    store_planes(second_ref, packed_ref, odd)


def store_turned(total_ref, product, offset, first_row, channels):
    rows = product.shape[0]
    spare = LANES - channels
    group, place = divmod(offset, 4)
    if place < 3:
        base = first_row + (3 * group + place) * rows
        total_ref[pl.ds(base, rows), :channels] = product[:, :channels]
    else:
        for piece in range(3):
            base = first_row + (3 * group + piece) * rows
            total_ref[pl.ds(base, rows), channels:] = product[:, piece * spare : (piece + 1) * spare]


TAPS = range(27)
CHUNKS = [TAPS[first : first + 6] for first in range(0, 27, 6)]


def offset_of(tap):
    return 9 * (tap % 3) + tap // 3


def staged(target, tap, count, more=0):
    code, dx = divmod(tap, 3)
    dy, dz = divmod(code, 3)
    row = 16 * ((dy + more) // 2)
    first = dx + more
    block = target[dz, (dy + more) % 2, first : first + count, row : row + 8 * count, :]
    return block.reshape(8 * count * count, target.shape[4])


def main_kernel(
    neighbors_ref, own_ref, partner_ref, first_ref, second_ref, first_far_ref, second_far_ref,
    turned_ref, one_ref, two_ref, output_ref, kept_p_ref, kept_q_ref, sent_p_ref, sent_q_ref,
    masked_w, grad_w, hidden_w, total, masked_s, plane_s, hidden_s, grad_s,
):
    odd, split = lax.axis_index("region") % 2, lax.axis_index("split")
    channels = one_ref.shape[2]
    wide = grad_w.shape[3]
    outs = turned_ref.shape[0]
    masked_w[:, 6:18] = jnp.zeros((12, 12, 24, LANES), F32)
    grad_w[:, 7:17] = jnp.zeros((10, 10, 24, wide), F32)

    own = own_ref[...].astype(F32).reshape(8, 8, 8, LANES + wide)
    masked_w[2:10, 8:16, 8:16, :] = own[..., :LANES]
    grad_w[1:9, 8:16, 8:16, :] = own[..., LANES:]

    def placed(step_x, step_z):
        found = [neighbors_ref[0, 9 * (step_x + 1) + 3 * step_y + step_z + 1] >= 0 for step_y in range(3)]
        y = jnp.where(found[0], 0, jnp.where(found[1], 1, 2))
        return found[0] | found[1] | found[2], pl.multiple_of(8 * y, 8)

    step_z = 1 - 2 * split
    valid, y = placed(0, step_z)
    z = pl.multiple_of(8 + 8 * step_z, 8)

    @pl.when(valid)
    def _():
        block = partner_ref[...].astype(F32).reshape(8, 8, 8, LANES + wide)
        masked_w[2:10, pl.ds(y, 8), pl.ds(z, 8), :] = block[..., :LANES]
        grad_w[1:9, pl.ds(y, 8), pl.ds(z, 8), :] = block[..., LANES:]

    for which, refs in enumerate(((first_ref, first_far_ref), (second_ref, second_far_ref))):
        step_x = 1 - 2 * odd if which == 0 else 2 * odd - 1
        for source, ref in enumerate(refs):
            step_z = 0 if source == 0 else 1 - 2 * split
            valid, y = placed(step_x, step_z)
            z = pl.multiple_of(8 + 8 * step_z, 8)
            x_masked = jnp.where(step_x > 0, 10, 0)
            x_grad = jnp.where(step_x > 0, 9, 0)

            @pl.when(valid)
            def _():
                block = ref[...].astype(F32)
                masked_w[pl.ds(x_masked, 2), pl.ds(y, 8), pl.ds(z, 8), :] = block[:, :LANES].reshape(2, 8, 8, LANES)
                near = jnp.concatenate([block[:64, LANES:], block[64:, LANES:]], 1)
                grad_w[pl.ds(x_grad, 1), pl.ds(y, 8), pl.ds(z, 8), :] = near.reshape(1, 8, 8, wide)

    def stage(target, source, first_x, first_y, first_z):
        count_x, rows = target.shape[2:4]
        lanes = target.shape[4]
        for dz in range(3):
            block = source[
                first_x : first_x + count_x, first_y : first_y + rows // 8, first_z + dz : first_z + dz + 8, :
            ]
            target[dz, 0] = block.reshape(count_x, rows, lanes).astype(BF16)
            target[dz, 1, :, : rows - 16] = block[:, 1 : rows // 8 - 1].reshape(count_x, rows - 16, lanes).astype(BF16)

    beside = 16 - 9 * split
    stage(masked_s, masked_w, 0, 6, 7)
    for dz in range(3):
        plane = masked_w[:, 6:24, pl.ds(beside - 1 + dz, 1), :].reshape(12, 18, LANES)
        for dy in range(3):
            plane_s[dz, dy] = plane[:, dy : dy + 16, :].astype(BF16)
        if dz == 1:
            plane_flag = plane[1:11, 1:17, channels : channels + 1].reshape(160, 1) > 0

    def plane_rows(tap):
        code, dx = divmod(tap, 3)
        dy, dz = divmod(code, 3)
        return plane_s[dz, dy, dx : dx + 10].reshape(160, LANES)

    hidden_pre = None
    for chunk in CHUNKS:
        rows = jnp.concatenate(
            [jnp.concatenate([staged(masked_s, tap, 10), plane_rows(tap)], 0) for tap in chunk], 1
        )
        kernel = jnp.concatenate([one_ref[offset_of(tap)] for tap in chunk], 0)
        term = jnp.dot(rows, kernel, preferred_element_type=F32)
        hidden_pre = term if hidden_pre is None else hidden_pre + term
    flags = masked_w[1:11, 7:17, 8:16, channels : channels + 1].reshape(800, 1) > 0
    hidden_pre = jnp.where(jnp.concatenate([flags, plane_flag], 0), hidden_pre, 0.0)
    hidden = hidden_pre * jax.nn.sigmoid(hidden_pre)
    hidden = jnp.concatenate([hidden, jnp.zeros((960, LANES - channels), F32)], 1)
    hidden_w[:, :, 8:16, :] = hidden[:800].reshape(10, 10, 8, LANES)
    hidden_w[:, :, 0:8, :] = jnp.zeros((10, 10, 8, LANES), F32)
    hidden_w[:, :, 16:24, :] = jnp.zeros((10, 10, 8, LANES), F32)
    hidden_w[:, :, pl.ds(beside, 1), :] = hidden[800:].reshape(10, 16, LANES)[:, :10].reshape(10, 10, 1, LANES)
    own_pre = hidden_pre[:800].reshape(10, 10, 8, channels)[1:9, 1:9].reshape(512, channels)
    own_flag = masked_w[2:10, 8:16, 8:16, channels : channels + 1].reshape(512, 1) > 0

    first_one = 3 * (-(-27 // 4)) * outs
    turned_out = turned_ref[...]
    spare_rows = 3 * (-(-27 // 4) - 1)
    total[spare_rows * outs : first_one, channels:] = jnp.zeros((3 * outs, LANES - channels), F32)
    total[first_one + spare_rows * channels : first_one + (spare_rows + 3) * channels, channels:] = jnp.zeros(
        (3 * channels, LANES - channels), F32
    )
    stage(hidden_s, hidden_w, 0, 0, 7)
    output = None
    for chunk in CHUNKS:
        rows = jnp.concatenate([staged(hidden_s, tap, 8) for tap in chunk], 1)
        kernel = jnp.concatenate([two_ref[offset_of(tap)] for tap in chunk], 0)[:, :outs]
        term = jnp.dot(rows, kernel, preferred_element_type=F32)
        output = term if output is None else output + term
        product = jnp.dot(turned_out, rows, preferred_element_type=F32)
        for place, tap in enumerate(chunk):
            store_turned(total, product[:, place * LANES : (place + 1) * LANES], offset_of(tap), 0, channels)

    output_ref[...] = jnp.where(own_flag, output, 0.0).T.astype(BF16)

    stage(grad_s, grad_w, 0, 7, 7)
    back = None
    for chunk in CHUNKS:
        rows = jnp.concatenate([staged(grad_s, tap, 8) for tap in chunk], 1)
        kernel = jnp.concatenate([two_ref[26 - offset_of(tap)] for tap in chunk], 1)
        term = lax.dot_general(rows, kernel, (((1,), (1,)), ((), ())), preferred_element_type=F32)
        back = term if back is None else back + term
    back = back[:, :channels]
    gate = jax.nn.sigmoid(own_pre)
    grad_pre = jnp.where(own_flag, back * gate * (1.0 + own_pre * (1.0 - gate)), 0.0)
    turned_pre = grad_pre.T.astype(BF16)

    for chunk in CHUNKS:
        rows = jnp.concatenate([staged(masked_s, tap, 8, 1) for tap in chunk], 1)
        product = jnp.dot(turned_pre, rows, preferred_element_type=F32)
        for place, tap in enumerate(chunk):
            store_turned(
                total, product[:, place * LANES : (place + 1) * LANES], offset_of(tap), first_one, channels
            )

    half = kept_p_ref.shape[0]
    for start, kept_ref, sent_ref in ((0, kept_p_ref, sent_p_ref), (2 * half, kept_q_ref, sent_q_ref)):
        kept_ref[...] = total[pl.ds(pl.multiple_of(start + split * half, 16), half), :]
        sent_ref[...] = total[pl.ds(pl.multiple_of(start + (1 - split) * half, 16), half), :].astype(BF16)


def assemble(sums, start, own_ref, other_ref):
    split = lax.axis_index("split")
    half = own_ref.shape[0]
    sums[pl.ds(pl.multiple_of(start + split * half, 16), half), :] = own_ref[...]
    sums[pl.ds(pl.multiple_of(start + (1 - split) * half, 16), half), :] = other_ref[...]


def unpack(sums, first, groups, ref, target, sems):
    offsets, channels, outs = ref.shape
    row = lax.broadcasted_iota(jnp.int32, (LANES, LANES), 0)
    unit = jnp.where(row == lax.broadcasted_iota(jnp.int32, (LANES, LANES), 1), 1.0, 0.0).astype(BF16)
    spare = LANES - channels
    copies = []
    for group in groups:
        for place in range(3):
            part = sums[pl.ds(first + (3 * group + place) * outs, outs), :]
            part = lax.dot_general(unit, part, (((1,), (1,)), ((), ())), preferred_element_type=F32)
            ref[4 * group + place] = part[:channels]
            if 4 * group + 3 < offsets:
                ref[4 * group + 3, place * spare : (place + 1) * spare, :] = part[channels:]
        done = pl.ds(4 * group, min(4, offsets - 4 * group))
        copies.append(pltpu.make_async_copy(ref.at[done], target.at[done], sems.at[len(copies)]))
        copies[-1].start()
    return copies


def first_unpack_kernel(groups, own_ref, other_ref, two_hbm, sums, two_ref, sems):
    assemble(sums, 0, own_ref, other_ref)
    for copy in unpack(sums, 0, groups, two_ref, two_hbm, sems):
        copy.wait()


def second_unpack_kernel(
    groups, own_p_ref, other_p_ref, own_q_ref, other_q_ref, _, one_hbm, two_hbm, sums, one_ref, two_ref, one_sems, two_sems
):
    offsets, _, outs = two_ref.shape
    assemble(sums, 0, own_p_ref, other_p_ref)
    assemble(sums, 2 * own_p_ref.shape[0], own_q_ref, other_q_ref)
    fours = -(-offsets // 4)
    copies = unpack(sums, 0, groups, two_ref, two_hbm, two_sems)
    copies += unpack(sums, 3 * fours * outs, range(fours), one_ref, one_hbm, one_sems)
    for copy in copies:
        copy.wait()


def call(kernel, out_shape, args, scalars=0, scratch=(), cost=None, into=pltpu.VMEM, mib=12, filled=False):
    spaces = [pltpu.SMEM] * scalars + [pltpu.VMEM] * (len(args) - scalars)
    if filled:
        spaces[-1] = into
    return pl.pallas_call(
        kernel,
        out_shape=out_shape,
        in_specs=[pl.BlockSpec(memory_space=space) for space in spaces],
        out_specs=jax.tree.map(lambda _: pl.BlockSpec(memory_space=into), out_shape),
        scratch_shapes=list(scratch),
        compiler_params=pltpu.CompilerParams(vmem_limit_bytes=mib * 2**20),
        cost_estimate=cost,
        input_output_aliases={len(args) - 1: len(out_shape) - 1} if filled else {},
    )(*args)


def exchanged(value, axis, mask):
    return lax.ppermute(value, axis, [(i, i ^ mask) for i in range(lax.axis_size(axis))])


def halves(value, bit):
    half = value.shape[0] // 2
    return (
        lax.dynamic_slice_in_dim(value, bit * half, half, 0),
        lax.dynamic_slice_in_dim(value, (1 - bit) * half, half, 0),
    )


def shards(features, kernel_one, kernel_two, occupancy, neighbors, cotangent):
    channels, voxels = features.shape
    offsets, _, outs = kernel_two.shape
    regions = lax.axis_size("region")
    region = lax.axis_index("region").astype(jnp.int32)
    split = lax.axis_index("split").astype(jnp.int32)
    wide = up_to(outs, LANES)
    struct = jax.ShapeDtypeStruct

    spare = LANES - channels
    stack = jnp.pad(features, ((0, spare + wide), (0, 0))) + jnp.pad(cotangent, ((LANES, wide - outs), (0, 0)))
    planes = struct((128, 2 * LANES), BF16)
    packed, first, second, turned = call(
        functools.partial(pack_kernel, channels),
        (struct((voxels, LANES + wide), BF16), planes, planes, struct((outs, voxels), BF16)),
        (stack, occupancy),
    )
    pairs = [(i, i + 1) for i in range(1, regions - 1, 2)]
    second = lax.ppermute(second, "region", pairs + [(b, a) for a, b in pairs])
    first = lax.ppermute(first, "region", [(i, i ^ 1) for i in range(regions)])
    partner = exchanged(packed, "split", 1)
    one = jnp.pad(kernel_one, ((0, 0), (0, LANES - channels), (0, 0)))
    two = jnp.pad(kernel_two, ((0, 0), (0, LANES - channels), (0, wide - outs)))
    second, one, two = lax.optimization_barrier((second, one, two))
    second_far = exchanged(second, "split", 1)
    first_far = exchanged(first, "split", 1)

    tile_rows = 3 * -(-offsets // 4) * (outs + channels)
    half = up_to(tile_rows, 4 * regions * 8) // 4
    kept, sent = struct((half, LANES), F32), struct((half, LANES), BF16)
    output, *sums = call(
        main_kernel,
        (struct((outs, voxels), BF16), kept, kept, sent, sent),
        (neighbors, packed, partner, first, second, first_far, second_far, turned, one, two),
        scalars=1,
        mib=26,
        scratch=(
            pltpu.VMEM((12, 24, 24, LANES), F32),
            pltpu.VMEM((10, 24, 24, wide), F32),
            pltpu.VMEM((10, 10, 24, LANES), F32),
            pltpu.VMEM((4 * half, LANES), F32),
            pltpu.VMEM((3, 2, 12, 96, LANES), BF16),
            pltpu.VMEM((3, 3, 12, 16, LANES), BF16),
            pltpu.VMEM((3, 2, 10, 80, LANES), BF16),
            pltpu.VMEM((3, 2, 10, 80, wide), BF16),
        ),
    )
    sums = [sums[part] + exchanged(sums[2 + part], "split", 1).astype(F32) for part in range(2)]
    bits = list(range((regions - 1).bit_length()))
    orders = [bits[:-2] + bits[:-3:-1], bits[1::-1] + bits[2:]]
    whole_steps = 2

    for step in range(len(bits) - whole_steps):
        for part, order in enumerate(orders):
            mask = 1 << order[step]
            keep, give = halves(sums[part], (region // mask) % 2)
            sums[part] = keep + exchanged(give.astype(BF16), "region", mask).astype(F32)
    for step in range(len(bits) - whole_steps, len(bits)):
        for part, order in enumerate(orders):
            own = sums[part].astype(BF16)
            sums[part] = own.astype(F32) + exchanged(own, "region", 1 << order[step]).astype(F32)
    sums = [value.astype(BF16) for value in sums]

    def joined(own, other, bit):
        return jnp.where(bit == 0, jnp.concatenate([own, other], 0), jnp.concatenate([other, own], 0))

    for step in reversed(range(len(bits) - whole_steps)):
        for part, order in enumerate(orders):
            mask = 1 << order[step]
            sums[part] = joined(sums[part], exchanged(sums[part], "region", mask), (region // mask) % 2)
    ends = [(own, exchanged(own, "split", 1)) for own in sums]
    fours = -(-offsets // 4)
    early = min(fours, 2 * half // (3 * outs))
    one_shape, two_shape = struct((offsets, channels, channels), F32), struct((offsets, channels, outs), F32)
    grad_two = call(
        functools.partial(first_unpack_kernel, range(early)),
        two_shape,
        ends[0],
        scratch=(
            pltpu.VMEM((2 * half, LANES), BF16),
            pltpu.VMEM(two_shape.shape, F32),
            pltpu.SemaphoreType.DMA((fours,)),
        ),
        cost=pl.CostEstimate(flops=10**8, bytes_accessed=4 * 2**20, transcendentals=0),
        into=pltpu.HBM,
    )
    grad_one, grad_two = call(
        functools.partial(second_unpack_kernel, range(early, fours)),
        (one_shape, two_shape),
        (*ends[0], *ends[1], grad_two),
        scratch=(
            pltpu.VMEM((4 * half, LANES), BF16),
            pltpu.VMEM(one_shape.shape, F32),
            pltpu.VMEM(two_shape.shape, F32),
            pltpu.SemaphoreType.DMA((fours,)),
            pltpu.SemaphoreType.DMA((fours,)),
        ),
        into=pltpu.HBM,
        filled=True,
    )
    return output, grad_one, grad_two


def solution(mesh):
    rows = P(("region", "split"), None)
    columns = P(None, ("region", "split"))
    return jax.shard_map(
        shards,
        mesh=mesh,
        in_specs=(columns, P(), P(), rows, rows, columns),
        out_specs=(columns, P(), P()),
        check_vma=False,
    )
```

```python
import functools

import jax
import jax.numpy as jnp
from jax import lax
from jax.experimental import pallas as pl
from jax.experimental.pallas import tpu as pltpu
from jax.sharding import PartitionSpec as P

F32 = jnp.float32
BF16 = jnp.bfloat16
LANES = 128


def up_to(value, step):
    return -(-value // step) * step


def store_planes(target_ref, rows, upper):
    row = pl.multiple_of(upper * 384, 128)
    near = pl.multiple_of(upper * 448, 64)
    target_ref[:, :LANES] = rows[pl.ds(row, 128), :LANES]
    target_ref[:64, LANES:] = rows[pl.ds(near, 64), LANES : 2 * LANES]
    target_ref[64:, LANES:] = rows[pl.ds(near, 64), 2 * LANES :]


def pack_kernel(channels, stack_ref, occupancy_ref, packed_ref, first_ref, second_ref, turned_ref):
    active = occupancy_ref[...] > 0
    row = lax.broadcasted_iota(jnp.int32, stack_ref.shape, 0)
    masked = jnp.where(active, jnp.where(row == channels, 1.0, stack_ref[...].astype(F32)), 0.0)
    packed_ref[...] = masked.T.astype(BF16)
    turned_ref[...] = masked[LANES : LANES + turned_ref.shape[0]].astype(BF16)
    odd = lax.axis_index("region") % 2
    store_planes(first_ref, packed_ref, 1 - odd)
    store_planes(second_ref, packed_ref, odd)


def store_turned(total_ref, product, offset, first_row, channels):
    rows = product.shape[0]
    spare = LANES - channels
    group, place = divmod(offset, 4)
    if place < 3:
        base = first_row + (3 * group + place) * rows
        total_ref[pl.ds(base, rows), :channels] = product[:, :channels]
    else:
        for piece in range(3):
            base = first_row + (3 * group + piece) * rows
            total_ref[pl.ds(base, rows), channels:] = product[:, piece * spare : (piece + 1) * spare]


TAPS = range(27)
CHUNKS = [TAPS[first : first + 6] for first in range(0, 27, 6)]


def offset_of(tap):
    return 9 * (tap % 3) + tap // 3


def staged(target, tap, count, more=0):
    code, dx = divmod(tap, 3)
    dy, dz = divmod(code, 3)
    row = 16 * ((dy + more) // 2)
    first = dx + more
    block = target[dz, (dy + more) % 2, first : first + count, row : row + 8 * count, :]
    return block.reshape(8 * count * count, target.shape[4])


def main_kernel(
    neighbors_ref, own_ref, partner_ref, first_ref, second_ref, first_far_ref, second_far_ref,
    turned_ref, one_ref, two_ref, output_ref, kept_p_ref, kept_q_ref, sent_p_ref, sent_q_ref,
    masked_w, grad_w, hidden_w, total, masked_s, plane_s, hidden_s, grad_s,
):
    odd, split = lax.axis_index("region") % 2, lax.axis_index("split")
    channels = one_ref.shape[2]
    wide = grad_w.shape[3]
    outs = turned_ref.shape[0]
    masked_w[:, 6:18] = jnp.zeros((12, 12, 24, LANES), F32)
    grad_w[:, 7:17] = jnp.zeros((10, 10, 24, wide), F32)

    own = own_ref[...].astype(F32).reshape(8, 8, 8, LANES + wide)
    masked_w[2:10, 8:16, 8:16, :] = own[..., :LANES]
    grad_w[1:9, 8:16, 8:16, :] = own[..., LANES:]

    def placed(step_x, step_z):
        found = [neighbors_ref[0, 9 * (step_x + 1) + 3 * step_y + step_z + 1] >= 0 for step_y in range(3)]
        y = jnp.where(found[0], 0, jnp.where(found[1], 1, 2))
        return found[0] | found[1] | found[2], pl.multiple_of(8 * y, 8)

    step_z = 1 - 2 * split
    valid, y = placed(0, step_z)
    z = pl.multiple_of(8 + 8 * step_z, 8)

    @pl.when(valid)
    def _():
        block = partner_ref[...].astype(F32).reshape(8, 8, 8, LANES + wide)
        masked_w[2:10, pl.ds(y, 8), pl.ds(z, 8), :] = block[..., :LANES]
        grad_w[1:9, pl.ds(y, 8), pl.ds(z, 8), :] = block[..., LANES:]

    for which, refs in enumerate(((first_ref, first_far_ref), (second_ref, second_far_ref))):
        step_x = 1 - 2 * odd if which == 0 else 2 * odd - 1
        for source, ref in enumerate(refs):
            step_z = 0 if source == 0 else 1 - 2 * split
            valid, y = placed(step_x, step_z)
            z = pl.multiple_of(8 + 8 * step_z, 8)
            x_masked = jnp.where(step_x > 0, 10, 0)
            x_grad = jnp.where(step_x > 0, 9, 0)

            @pl.when(valid)
            def _():
                block = ref[...].astype(F32)
                masked_w[pl.ds(x_masked, 2), pl.ds(y, 8), pl.ds(z, 8), :] = block[:, :LANES].reshape(2, 8, 8, LANES)
                near = jnp.concatenate([block[:64, LANES:], block[64:, LANES:]], 1)
                grad_w[pl.ds(x_grad, 1), pl.ds(y, 8), pl.ds(z, 8), :] = near.reshape(1, 8, 8, wide)

    def stage(target, source, first_x, first_y, first_z):
        count_x, rows = target.shape[2:4]
        lanes = target.shape[4]
        for dz in range(3):
            block = source[
                first_x : first_x + count_x, first_y : first_y + rows // 8, first_z + dz : first_z + dz + 8, :
            ]
            target[dz, 0] = block.reshape(count_x, rows, lanes).astype(BF16)
            target[dz, 1, :, : rows - 16] = block[:, 1 : rows // 8 - 1].reshape(count_x, rows - 16, lanes).astype(BF16)

    beside = 16 - 9 * split
    stage(masked_s, masked_w, 0, 6, 7)
    for dz in range(3):
        plane = masked_w[:, 6:24, pl.ds(beside - 1 + dz, 1), :].reshape(12, 18, LANES)
        for dy in range(3):
            plane_s[dz, dy] = plane[:, dy : dy + 16, :].astype(BF16)
        if dz == 1:
            plane_flag = plane[1:11, 1:17, channels : channels + 1].reshape(160, 1) > 0

    def plane_rows(tap):
        code, dx = divmod(tap, 3)
        dy, dz = divmod(code, 3)
        return plane_s[dz, dy, dx : dx + 10].reshape(160, LANES)

    hidden_pre = None
    for chunk in CHUNKS:
        rows = jnp.concatenate(
            [jnp.concatenate([staged(masked_s, tap, 10), plane_rows(tap)], 0) for tap in chunk], 1
        )
        kernel = jnp.concatenate([one_ref[offset_of(tap)] for tap in chunk], 0)
        term = jnp.dot(rows, kernel, preferred_element_type=F32)
        hidden_pre = term if hidden_pre is None else hidden_pre + term
    flags = masked_w[1:11, 7:17, 8:16, channels : channels + 1].reshape(800, 1) > 0
    hidden_pre = jnp.where(jnp.concatenate([flags, plane_flag], 0), hidden_pre, 0.0)
    hidden = hidden_pre * jax.nn.sigmoid(hidden_pre)
    hidden = jnp.concatenate([hidden, jnp.zeros((960, LANES - channels), F32)], 1)
    hidden_w[:, :, 8:16, :] = hidden[:800].reshape(10, 10, 8, LANES)
    hidden_w[:, :, 0:8, :] = jnp.zeros((10, 10, 8, LANES), F32)
    hidden_w[:, :, 16:24, :] = jnp.zeros((10, 10, 8, LANES), F32)
    hidden_w[:, :, pl.ds(beside, 1), :] = hidden[800:].reshape(10, 16, LANES)[:, :10].reshape(10, 10, 1, LANES)
    own_pre = hidden_pre[:800].reshape(10, 10, 8, channels)[1:9, 1:9].reshape(512, channels)
    own_flag = masked_w[2:10, 8:16, 8:16, channels : channels + 1].reshape(512, 1) > 0

    first_one = 3 * (-(-27 // 4)) * outs
    turned_out = turned_ref[...]
    spare_rows = 3 * (-(-27 // 4) - 1)
    total[spare_rows * outs : first_one, channels:] = jnp.zeros((3 * outs, LANES - channels), F32)
    total[first_one + spare_rows * channels : first_one + (spare_rows + 3) * channels, channels:] = jnp.zeros(
        (3 * channels, LANES - channels), F32
    )
    stage(hidden_s, hidden_w, 0, 0, 7)
    output = None
    for chunk in CHUNKS:
        rows = jnp.concatenate([staged(hidden_s, tap, 8) for tap in chunk], 1)
        kernel = jnp.concatenate([two_ref[offset_of(tap)] for tap in chunk], 0)[:, :outs]
        term = jnp.dot(rows, kernel, preferred_element_type=F32)
        output = term if output is None else output + term
        product = jnp.dot(turned_out, rows, preferred_element_type=F32)
        for place, tap in enumerate(chunk):
            store_turned(total, product[:, place * LANES : (place + 1) * LANES], offset_of(tap), 0, channels)

    output_ref[...] = jnp.where(own_flag, output, 0.0).T.astype(BF16)

    def hand_over(start, kept_ref, sent_ref):
        half = kept_ref.shape[0]
        kept_ref[...] = total[pl.ds(pl.multiple_of(start + split * half, 16), half), :]
        sent_ref[...] = total[pl.ds(pl.multiple_of(start + (1 - split) * half, 16), half), :].astype(BF16)

    hand_over(0, kept_p_ref, sent_p_ref)

    stage(grad_s, grad_w, 0, 7, 7)
    back = None
    for chunk in CHUNKS:
        rows = jnp.concatenate([staged(grad_s, tap, 8) for tap in chunk], 1)
        kernel = jnp.concatenate([two_ref[26 - offset_of(tap)] for tap in chunk], 1)
        term = lax.dot_general(rows, kernel, (((1,), (1,)), ((), ())), preferred_element_type=F32)
        back = term if back is None else back + term
    back = back[:, :channels]
    gate = jax.nn.sigmoid(own_pre)
    grad_pre = jnp.where(own_flag, back * gate * (1.0 + own_pre * (1.0 - gate)), 0.0)
    turned_pre = grad_pre.T.astype(BF16)

    for chunk in CHUNKS:
        rows = jnp.concatenate([staged(masked_s, tap, 8, 1) for tap in chunk], 1)
        product = jnp.dot(turned_pre, rows, preferred_element_type=F32)
        for place, tap in enumerate(chunk):
            store_turned(
                total, product[:, place * LANES : (place + 1) * LANES], offset_of(tap), first_one, channels
            )

    hand_over(2 * kept_p_ref.shape[0], kept_q_ref, sent_q_ref)


def assemble(sums, start, own_ref, other_ref):
    split = lax.axis_index("split")
    half = own_ref.shape[0]
    sums[pl.ds(pl.multiple_of(start + split * half, 16), half), :] = own_ref[...]
    sums[pl.ds(pl.multiple_of(start + (1 - split) * half, 16), half), :] = other_ref[...]


def unpack(sums, first, groups, ref, target, sems):
    offsets, channels, outs = ref.shape
    row = lax.broadcasted_iota(jnp.int32, (LANES, LANES), 0)
    unit = jnp.where(row == lax.broadcasted_iota(jnp.int32, (LANES, LANES), 1), 1.0, 0.0).astype(BF16)
    spare = LANES - channels
    copies = []
    for group in groups:
        for place in range(3):
            part = sums[pl.ds(first + (3 * group + place) * outs, outs), :]
            part = lax.dot_general(unit, part, (((1,), (1,)), ((), ())), preferred_element_type=F32)
            ref[4 * group + place] = part[:channels]
            if 4 * group + 3 < offsets:
                ref[4 * group + 3, place * spare : (place + 1) * spare, :] = part[channels:]
        done = pl.ds(4 * group, min(4, offsets - 4 * group))
        copies.append(pltpu.make_async_copy(ref.at[done], target.at[done], sems.at[len(copies)]))
        copies[-1].start()
    return copies


def first_unpack_kernel(groups, own_ref, other_ref, two_hbm, sums, two_ref, sems):
    assemble(sums, 0, own_ref, other_ref)
    for copy in unpack(sums, 0, groups, two_ref, two_hbm, sems):
        copy.wait()


def second_unpack_kernel(
    groups, own_p_ref, other_p_ref, own_q_ref, other_q_ref, _, one_hbm, two_hbm, sums, one_ref, two_ref, one_sems, two_sems
):
    offsets, _, outs = two_ref.shape
    assemble(sums, 0, own_p_ref, other_p_ref)
    assemble(sums, 2 * own_p_ref.shape[0], own_q_ref, other_q_ref)
    fours = -(-offsets // 4)
    copies = unpack(sums, 0, groups, two_ref, two_hbm, two_sems)
    copies += unpack(sums, 3 * fours * outs, range(fours), one_ref, one_hbm, one_sems)
    for copy in copies:
        copy.wait()


def call(kernel, out_shape, args, scalars=0, scratch=(), cost=None, into=pltpu.VMEM, mib=12, filled=False):
    spaces = [pltpu.SMEM] * scalars + [pltpu.VMEM] * (len(args) - scalars)
    if filled:
        spaces[-1] = into
    return pl.pallas_call(
        kernel,
        out_shape=out_shape,
        in_specs=[pl.BlockSpec(memory_space=space) for space in spaces],
        out_specs=jax.tree.map(lambda _: pl.BlockSpec(memory_space=into), out_shape),
        scratch_shapes=list(scratch),
        compiler_params=pltpu.CompilerParams(vmem_limit_bytes=mib * 2**20),
        cost_estimate=cost,
        input_output_aliases={len(args) - 1: len(out_shape) - 1} if filled else {},
    )(*args)


def exchanged(value, axis, mask):
    return lax.ppermute(value, axis, [(i, i ^ mask) for i in range(lax.axis_size(axis))])


def halves(value, bit):
    half = value.shape[0] // 2
    return (
        lax.dynamic_slice_in_dim(value, bit * half, half, 0),
        lax.dynamic_slice_in_dim(value, (1 - bit) * half, half, 0),
    )


def shards(features, kernel_one, kernel_two, occupancy, neighbors, cotangent):
    channels, voxels = features.shape
    offsets, _, outs = kernel_two.shape
    regions = lax.axis_size("region")
    region = lax.axis_index("region").astype(jnp.int32)
    split = lax.axis_index("split").astype(jnp.int32)
    wide = up_to(outs, LANES)
    struct = jax.ShapeDtypeStruct

    spare = LANES - channels
    stack = jnp.pad(features, ((0, spare + wide), (0, 0))) + jnp.pad(cotangent, ((LANES, wide - outs), (0, 0)))
    planes = struct((128, 2 * LANES), BF16)
    packed, first, second, turned = call(
        functools.partial(pack_kernel, channels),
        (struct((voxels, LANES + wide), BF16), planes, planes, struct((outs, voxels), BF16)),
        (stack, occupancy),
    )
    pairs = [(i, i + 1) for i in range(1, regions - 1, 2)]
    second = lax.ppermute(second, "region", pairs + [(b, a) for a, b in pairs])
    first = lax.ppermute(first, "region", [(i, i ^ 1) for i in range(regions)])
    partner = exchanged(packed, "split", 1)
    one = jnp.pad(kernel_one, ((0, 0), (0, LANES - channels), (0, 0)))
    two = jnp.pad(kernel_two, ((0, 0), (0, LANES - channels), (0, wide - outs)))
    second, one, two = lax.optimization_barrier((second, one, two))
    second_far = exchanged(second, "split", 1)
    first_far = exchanged(first, "split", 1)

    tile_rows = 3 * -(-offsets // 4) * (outs + channels)
    half = up_to(tile_rows, 4 * regions * 8) // 4
    kept, sent = struct((half, LANES), F32), struct((half, LANES), BF16)
    output, *sums = call(
        main_kernel,
        (struct((outs, voxels), BF16), kept, kept, sent, sent),
        (neighbors, packed, partner, first, second, first_far, second_far, turned, one, two),
        scalars=1,
        mib=26,
        scratch=(
            pltpu.VMEM((12, 24, 24, LANES), F32),
            pltpu.VMEM((10, 24, 24, wide), F32),
            pltpu.VMEM((10, 10, 24, LANES), F32),
            pltpu.VMEM((4 * half, LANES), F32),
            pltpu.VMEM((3, 2, 12, 96, LANES), BF16),
            pltpu.VMEM((3, 3, 12, 16, LANES), BF16),
            pltpu.VMEM((3, 2, 10, 80, LANES), BF16),
            pltpu.VMEM((3, 2, 10, 80, wide), BF16),
        ),
    )
    sums = [sums[part] + exchanged(sums[2 + part], "split", 1).astype(F32) for part in range(2)]
    bits = list(range((regions - 1).bit_length()))
    orders = [bits[:-2] + bits[:-3:-1], bits[1::-1] + bits[2:]]
    whole_steps = 2

    for step in range(len(bits) - whole_steps):
        for part, order in enumerate(orders):
            mask = 1 << order[step]
            keep, give = halves(sums[part], (region // mask) % 2)
            sums[part] = keep + exchanged(give.astype(BF16), "region", mask).astype(F32)
    for step in range(len(bits) - whole_steps, len(bits)):
        for part, order in enumerate(orders):
            own = sums[part].astype(BF16)
            sums[part] = own.astype(F32) + exchanged(own, "region", 1 << order[step]).astype(F32)
    sums = [value.astype(BF16) for value in sums]

    def joined(own, other, bit):
        return jnp.where(bit == 0, jnp.concatenate([own, other], 0), jnp.concatenate([other, own], 0))

    for step in reversed(range(len(bits) - whole_steps)):
        for part, order in enumerate(orders):
            mask = 1 << order[step]
            sums[part] = joined(sums[part], exchanged(sums[part], "region", mask), (region // mask) % 2)
    ends = [(own, exchanged(own, "split", 1)) for own in sums]
    fours = -(-offsets // 4)
    early = min(fours, 2 * half // (3 * outs))
    one_shape, two_shape = struct((offsets, channels, channels), F32), struct((offsets, channels, outs), F32)
    grad_two = call(
        functools.partial(first_unpack_kernel, range(early)),
        two_shape,
        ends[0],
        scratch=(
            pltpu.VMEM((2 * half, LANES), BF16),
            pltpu.VMEM(two_shape.shape, F32),
            pltpu.SemaphoreType.DMA((fours,)),
        ),
        cost=pl.CostEstimate(flops=10**8, bytes_accessed=4 * 2**20, transcendentals=0),
        into=pltpu.HBM,
    )
    grad_one, grad_two = call(
        functools.partial(second_unpack_kernel, range(early, fours)),
        (one_shape, two_shape),
        (*ends[0], *ends[1], grad_two),
        scratch=(
            pltpu.VMEM((4 * half, LANES), BF16),
            pltpu.VMEM(one_shape.shape, F32),
            pltpu.VMEM(two_shape.shape, F32),
            pltpu.SemaphoreType.DMA((fours,)),
            pltpu.SemaphoreType.DMA((fours,)),
        ),
        into=pltpu.HBM,
        filled=True,
    )
    return output, grad_one, grad_two


def solution(mesh):
    rows = P(("region", "split"), None)
    columns = P(None, ("region", "split"))
    return jax.shard_map(
        shards,
        mesh=mesh,
        in_specs=(columns, P(), P(), rows, rows, columns),
        out_specs=(columns, P(), P()),
        check_vma=False,
    )
```

```python
import functools

import jax
import jax.numpy as jnp
from jax import lax
from jax.experimental import pallas as pl
from jax.experimental.pallas import tpu as pltpu
from jax.sharding import PartitionSpec as P

F32 = jnp.float32
BF16 = jnp.bfloat16
LANES = 128


def up_to(value, step):
    return -(-value // step) * step


def store_planes(target_ref, rows, upper):
    row = pl.multiple_of(upper * 384, 128)
    near = pl.multiple_of(upper * 448, 64)
    target_ref[:, :LANES] = rows[pl.ds(row, 128), :LANES]
    target_ref[:64, LANES:] = rows[pl.ds(near, 64), LANES : 2 * LANES]
    target_ref[64:, LANES:] = rows[pl.ds(near, 64), 2 * LANES :]


def pack_kernel(channels, stack_ref, occupancy_ref, packed_ref, first_ref, second_ref, turned_ref):
    active = occupancy_ref[...] > 0
    row = lax.broadcasted_iota(jnp.int32, stack_ref.shape, 0)
    masked = jnp.where(active, jnp.where(row == channels, 1.0, stack_ref[...].astype(F32)), 0.0)
    packed_ref[...] = masked.T.astype(BF16)
    turned_ref[...] = masked[LANES : LANES + turned_ref.shape[0]].astype(BF16)
    odd = lax.axis_index("region") % 2
    store_planes(first_ref, packed_ref, 1 - odd)
    store_planes(second_ref, packed_ref, odd)


def store_turned(total_ref, product, offset, first_row, channels):
    rows = product.shape[0]
    spare = LANES - channels
    group, place = divmod(offset, 4)
    if place < 3:
        base = first_row + (3 * group + place) * rows
        total_ref[pl.ds(base, rows), :channels] = product[:, :channels]
    else:
        for piece in range(3):
            base = first_row + (3 * group + piece) * rows
            total_ref[pl.ds(base, rows), channels:] = product[:, piece * spare : (piece + 1) * spare]


TAPS = range(27)
CHUNKS = [TAPS[first : first + 6] for first in range(0, 27, 6)]


def offset_of(tap):
    return 9 * (tap % 3) + tap // 3


def staged(target, tap, count, more=0):
    code, dx = divmod(tap, 3)
    dy, dz = divmod(code, 3)
    row = 16 * ((dy + more) // 2)
    first = dx + more
    block = target[dz, (dy + more) % 2, first : first + count, row : row + 8 * count, :]
    return block.reshape(8 * count * count, target.shape[4])


def main_kernel(
    neighbors_ref, own_ref, partner_ref, first_ref, second_ref, first_far_ref, second_far_ref,
    turned_ref, one_ref, two_ref, output_ref, kept_p_ref, kept_q_ref, kept_r_ref, sent_p_ref, sent_q_ref, sent_r_ref,
    masked_w, grad_w, hidden_w, total, masked_s, plane_s, hidden_s, grad_s,
):
    odd, split = lax.axis_index("region") % 2, lax.axis_index("split")
    channels = one_ref.shape[2]
    wide = grad_w.shape[3]
    outs = turned_ref.shape[0]
    masked_w[:, 6:18] = jnp.zeros((12, 12, 24, LANES), F32)
    grad_w[:, 7:17] = jnp.zeros((10, 10, 24, wide), F32)

    own = own_ref[...].astype(F32).reshape(8, 8, 8, LANES + wide)
    masked_w[2:10, 8:16, 8:16, :] = own[..., :LANES]
    grad_w[1:9, 8:16, 8:16, :] = own[..., LANES:]

    def placed(step_x, step_z):
        found = [neighbors_ref[0, 9 * (step_x + 1) + 3 * step_y + step_z + 1] >= 0 for step_y in range(3)]
        y = jnp.where(found[0], 0, jnp.where(found[1], 1, 2))
        return found[0] | found[1] | found[2], pl.multiple_of(8 * y, 8)

    step_z = 1 - 2 * split
    valid, y = placed(0, step_z)
    z = pl.multiple_of(8 + 8 * step_z, 8)

    @pl.when(valid)
    def _():
        block = partner_ref[...].astype(F32).reshape(8, 8, 8, LANES + wide)
        masked_w[2:10, pl.ds(y, 8), pl.ds(z, 8), :] = block[..., :LANES]
        grad_w[1:9, pl.ds(y, 8), pl.ds(z, 8), :] = block[..., LANES:]

    for which, refs in enumerate(((first_ref, first_far_ref), (second_ref, second_far_ref))):
        step_x = 1 - 2 * odd if which == 0 else 2 * odd - 1
        for source, ref in enumerate(refs):
            step_z = 0 if source == 0 else 1 - 2 * split
            valid, y = placed(step_x, step_z)
            z = pl.multiple_of(8 + 8 * step_z, 8)
            x_masked = jnp.where(step_x > 0, 10, 0)
            x_grad = jnp.where(step_x > 0, 9, 0)

            @pl.when(valid)
            def _():
                block = ref[...].astype(F32)
                masked_w[pl.ds(x_masked, 2), pl.ds(y, 8), pl.ds(z, 8), :] = block[:, :LANES].reshape(2, 8, 8, LANES)
                near = jnp.concatenate([block[:64, LANES:], block[64:, LANES:]], 1)
                grad_w[pl.ds(x_grad, 1), pl.ds(y, 8), pl.ds(z, 8), :] = near.reshape(1, 8, 8, wide)

    def stage(target, source, first_x, first_y, first_z):
        count_x, rows = target.shape[2:4]
        lanes = target.shape[4]
        for dz in range(3):
            block = source[
                first_x : first_x + count_x, first_y : first_y + rows // 8, first_z + dz : first_z + dz + 8, :
            ]
            target[dz, 0] = block.reshape(count_x, rows, lanes).astype(BF16)
            target[dz, 1, :, : rows - 16] = block[:, 1 : rows // 8 - 1].reshape(count_x, rows - 16, lanes).astype(BF16)

    beside = 16 - 9 * split
    stage(masked_s, masked_w, 0, 6, 7)
    for dz in range(3):
        plane = masked_w[:, 6:24, pl.ds(beside - 1 + dz, 1), :].reshape(12, 18, LANES)
        for dy in range(3):
            plane_s[dz, dy] = plane[:, dy : dy + 16, :].astype(BF16)
        if dz == 1:
            plane_flag = plane[1:11, 1:17, channels : channels + 1].reshape(160, 1) > 0

    def plane_rows(tap):
        code, dx = divmod(tap, 3)
        dy, dz = divmod(code, 3)
        return plane_s[dz, dy, dx : dx + 10].reshape(160, LANES)

    hidden_pre = None
    for chunk in CHUNKS:
        rows = jnp.concatenate(
            [jnp.concatenate([staged(masked_s, tap, 10), plane_rows(tap)], 0) for tap in chunk], 1
        )
        kernel = jnp.concatenate([one_ref[offset_of(tap)] for tap in chunk], 0)
        term = jnp.dot(rows, kernel, preferred_element_type=F32)
        hidden_pre = term if hidden_pre is None else hidden_pre + term
    flags = masked_w[1:11, 7:17, 8:16, channels : channels + 1].reshape(800, 1) > 0
    hidden_pre = jnp.where(jnp.concatenate([flags, plane_flag], 0), hidden_pre, 0.0)
    hidden = hidden_pre * jax.nn.sigmoid(hidden_pre)
    hidden = jnp.concatenate([hidden, jnp.zeros((960, LANES - channels), F32)], 1)
    hidden_w[:, :, 8:16, :] = hidden[:800].reshape(10, 10, 8, LANES)
    hidden_w[:, :, 0:8, :] = jnp.zeros((10, 10, 8, LANES), F32)
    hidden_w[:, :, 16:24, :] = jnp.zeros((10, 10, 8, LANES), F32)
    hidden_w[:, :, pl.ds(beside, 1), :] = hidden[800:].reshape(10, 16, LANES)[:, :10].reshape(10, 10, 1, LANES)
    own_pre = hidden_pre[:800].reshape(10, 10, 8, channels)[1:9, 1:9].reshape(512, channels)
    own_flag = masked_w[2:10, 8:16, 8:16, channels : channels + 1].reshape(512, 1) > 0

    first_one = 3 * (-(-27 // 4)) * outs
    turned_out = turned_ref[...]
    spare_rows = 3 * (-(-27 // 4) - 1)
    total[spare_rows * outs : first_one, channels:] = jnp.zeros((3 * outs, LANES - channels), F32)
    total[first_one + spare_rows * channels : first_one + (spare_rows + 3) * channels, channels:] = jnp.zeros(
        (3 * channels, LANES - channels), F32
    )
    stage(hidden_s, hidden_w, 0, 0, 7)
    output = None
    for chunk in CHUNKS:
        rows = jnp.concatenate([staged(hidden_s, tap, 8) for tap in chunk], 1)
        kernel = jnp.concatenate([two_ref[offset_of(tap)] for tap in chunk], 0)[:, :outs]
        term = jnp.dot(rows, kernel, preferred_element_type=F32)
        output = term if output is None else output + term
        product = jnp.dot(turned_out, rows, preferred_element_type=F32)
        for place, tap in enumerate(chunk):
            store_turned(total, product[:, place * LANES : (place + 1) * LANES], offset_of(tap), 0, channels)

    output_ref[...] = jnp.where(own_flag, output, 0.0).T.astype(BF16)

    def hand_over(start, kept_ref, sent_ref):
        half = kept_ref.shape[0]
        kept_ref[...] = total[pl.ds(pl.multiple_of(start + split * half, 16), half), :]
        sent_ref[...] = total[pl.ds(pl.multiple_of(start + (1 - split) * half, 16), half), :].astype(BF16)

    hand_over(0, kept_p_ref, sent_p_ref)

    stage(grad_s, grad_w, 0, 7, 7)
    back = None
    for chunk in CHUNKS:
        rows = jnp.concatenate([staged(grad_s, tap, 8) for tap in chunk], 1)
        kernel = jnp.concatenate([two_ref[26 - offset_of(tap)] for tap in chunk], 1)
        term = lax.dot_general(rows, kernel, (((1,), (1,)), ((), ())), preferred_element_type=F32)
        back = term if back is None else back + term
    back = back[:, :channels]
    gate = jax.nn.sigmoid(own_pre)
    grad_pre = jnp.where(own_flag, back * gate * (1.0 + own_pre * (1.0 - gate)), 0.0)
    turned_pre = grad_pre.T.astype(BF16)

    for chunk in CHUNKS:
        rows = jnp.concatenate([staged(masked_s, tap, 8, 1) for tap in chunk], 1)
        product = jnp.dot(turned_pre, rows, preferred_element_type=F32)
        for place, tap in enumerate(chunk):
            store_turned(
                total, product[:, place * LANES : (place + 1) * LANES], offset_of(tap), first_one, channels
            )

    hand_over(2 * kept_p_ref.shape[0], kept_q_ref, sent_q_ref)
    hand_over(4 * kept_p_ref.shape[0], kept_r_ref, sent_r_ref)


def assemble(sums, start, own_ref, other_ref):
    split = lax.axis_index("split")
    half = own_ref.shape[0]
    sums[pl.ds(pl.multiple_of(start + split * half, 16), half), :] = own_ref[...]
    sums[pl.ds(pl.multiple_of(start + (1 - split) * half, 16), half), :] = other_ref[...]


def unpack(sums, first, groups, ref, target, sems):
    offsets, channels, outs = ref.shape
    row = lax.broadcasted_iota(jnp.int32, (LANES, LANES), 0)
    unit = jnp.where(row == lax.broadcasted_iota(jnp.int32, (LANES, LANES), 1), 1.0, 0.0).astype(BF16)
    spare = LANES - channels
    copies = []
    for group in groups:
        for place in range(3):
            part = sums[pl.ds(first + (3 * group + place) * outs, outs), :]
            part = lax.dot_general(unit, part, (((1,), (1,)), ((), ())), preferred_element_type=F32)
            ref[4 * group + place] = part[:channels]
            if 4 * group + 3 < offsets:
                ref[4 * group + 3, place * spare : (place + 1) * spare, :] = part[channels:]
        done = pl.ds(4 * group, min(4, offsets - 4 * group))
        copies.append(pltpu.make_async_copy(ref.at[done], target.at[done], sems.at[len(copies)]))
        copies[-1].start()
    return copies


def first_unpack_kernel(groups, own_ref, other_ref, two_hbm, sums, two_ref, sems):
    assemble(sums, 0, own_ref, other_ref)
    for copy in unpack(sums, 0, groups, two_ref, two_hbm, sems):
        copy.wait()


def second_unpack_kernel(
    groups, own_p_ref, other_p_ref, own_q_ref, other_q_ref, own_r_ref, other_r_ref, _, one_hbm, two_hbm, sums, one_ref, two_ref, one_sems, two_sems
):
    offsets, _, outs = two_ref.shape
    assemble(sums, 0, own_p_ref, other_p_ref)
    assemble(sums, 2 * own_p_ref.shape[0], own_q_ref, other_q_ref)
    assemble(sums, 4 * own_p_ref.shape[0], own_r_ref, other_r_ref)
    fours = -(-offsets // 4)
    copies = unpack(sums, 0, groups, two_ref, two_hbm, two_sems)
    copies += unpack(sums, 3 * fours * outs, range(fours), one_ref, one_hbm, one_sems)
    for copy in copies:
        copy.wait()


def call(kernel, out_shape, args, scalars=0, scratch=(), cost=None, into=pltpu.VMEM, mib=12, filled=False):
    spaces = [pltpu.SMEM] * scalars + [pltpu.VMEM] * (len(args) - scalars)
    if filled:
        spaces[-1] = into
    return pl.pallas_call(
        kernel,
        out_shape=out_shape,
        in_specs=[pl.BlockSpec(memory_space=space) for space in spaces],
        out_specs=jax.tree.map(lambda _: pl.BlockSpec(memory_space=into), out_shape),
        scratch_shapes=list(scratch),
        compiler_params=pltpu.CompilerParams(vmem_limit_bytes=mib * 2**20),
        cost_estimate=cost,
        input_output_aliases={len(args) - 1: len(out_shape) - 1} if filled else {},
    )(*args)


def exchanged(value, axis, mask):
    return lax.ppermute(value, axis, [(i, i ^ mask) for i in range(lax.axis_size(axis))])


def halves(value, bit):
    half = value.shape[0] // 2
    return (
        lax.dynamic_slice_in_dim(value, bit * half, half, 0),
        lax.dynamic_slice_in_dim(value, (1 - bit) * half, half, 0),
    )


def shards(features, kernel_one, kernel_two, occupancy, neighbors, cotangent):
    channels, voxels = features.shape
    offsets, _, outs = kernel_two.shape
    regions = lax.axis_size("region")
    region = lax.axis_index("region").astype(jnp.int32)
    split = lax.axis_index("split").astype(jnp.int32)
    wide = up_to(outs, LANES)
    struct = jax.ShapeDtypeStruct

    spare = LANES - channels
    stack = jnp.pad(features, ((0, spare + wide), (0, 0))) + jnp.pad(cotangent, ((LANES, wide - outs), (0, 0)))
    planes = struct((128, 2 * LANES), BF16)
    packed, first, second, turned = call(
        functools.partial(pack_kernel, channels),
        (struct((voxels, LANES + wide), BF16), planes, planes, struct((outs, voxels), BF16)),
        (stack, occupancy),
    )
    pairs = [(i, i + 1) for i in range(1, regions - 1, 2)]
    second = lax.ppermute(second, "region", pairs + [(b, a) for a, b in pairs])
    first = lax.ppermute(first, "region", [(i, i ^ 1) for i in range(regions)])
    partner = exchanged(packed, "split", 1)
    one = jnp.pad(kernel_one, ((0, 0), (0, LANES - channels), (0, 0)))
    two = jnp.pad(kernel_two, ((0, 0), (0, LANES - channels), (0, wide - outs)))
    second, one, two = lax.optimization_barrier((second, one, two))
    second_far = exchanged(second, "split", 1)
    first_far = exchanged(first, "split", 1)

    tile_rows = 3 * -(-offsets // 4) * (outs + channels)
    half = up_to(tile_rows, 6 * regions * 8) // 6
    kept, sent = struct((half, LANES), F32), struct((half, LANES), BF16)
    output, *sums = call(
        main_kernel,
        (struct((outs, voxels), BF16), *([kept] * 3), *([sent] * 3)),
        (neighbors, packed, partner, first, second, first_far, second_far, turned, one, two),
        scalars=1,
        mib=26,
        scratch=(
            pltpu.VMEM((12, 24, 24, LANES), F32),
            pltpu.VMEM((10, 24, 24, wide), F32),
            pltpu.VMEM((10, 10, 24, LANES), F32),
            pltpu.VMEM((6 * half, LANES), F32),
            pltpu.VMEM((3, 2, 12, 96, LANES), BF16),
            pltpu.VMEM((3, 3, 12, 16, LANES), BF16),
            pltpu.VMEM((3, 2, 10, 80, LANES), BF16),
            pltpu.VMEM((3, 2, 10, 80, wide), BF16),
        ),
    )
    sums = [sums[part] + exchanged(sums[3 + part], "split", 1).astype(F32) for part in range(3)]
    bits = list(range((regions - 1).bit_length()))
    orders = [bits[:-2] + bits[:-3:-1], bits[1::-1] + bits[2:], [2, 0] + bits[4:] + [3, 1]]
    whole_steps = 2

    for step in range(len(bits) - whole_steps):
        for part, order in enumerate(orders):
            mask = 1 << order[step]
            keep, give = halves(sums[part], (region // mask) % 2)
            sums[part] = keep + exchanged(give.astype(BF16), "region", mask).astype(F32)
    for step in range(len(bits) - whole_steps, len(bits)):
        for part, order in enumerate(orders):
            own = sums[part].astype(BF16)
            sums[part] = own.astype(F32) + exchanged(own, "region", 1 << order[step]).astype(F32)
    sums = [value.astype(BF16) for value in sums]

    def joined(own, other, bit):
        return jnp.where(bit == 0, jnp.concatenate([own, other], 0), jnp.concatenate([other, own], 0))

    for step in reversed(range(len(bits) - whole_steps)):
        for part, order in enumerate(orders):
            mask = 1 << order[step]
            sums[part] = joined(sums[part], exchanged(sums[part], "region", mask), (region // mask) % 2)
    ends = [(own, exchanged(own, "split", 1)) for own in sums]
    fours = -(-offsets // 4)
    early = min(fours, 2 * half // (3 * outs))
    one_shape, two_shape = struct((offsets, channels, channels), F32), struct((offsets, channels, outs), F32)
    grad_two = call(
        functools.partial(first_unpack_kernel, range(early)),
        two_shape,
        ends[0],
        scratch=(
            pltpu.VMEM((2 * half, LANES), BF16),
            pltpu.VMEM(two_shape.shape, F32),
            pltpu.SemaphoreType.DMA((fours,)),
        ),
        cost=pl.CostEstimate(flops=10**8, bytes_accessed=4 * 2**20, transcendentals=0),
        into=pltpu.HBM,
    )
    grad_one, grad_two = call(
        functools.partial(second_unpack_kernel, range(early, fours)),
        (one_shape, two_shape),
        (*ends[0], *ends[1], *ends[2], grad_two),
        scratch=(
            pltpu.VMEM((6 * half, LANES), BF16),
            pltpu.VMEM(one_shape.shape, F32),
            pltpu.VMEM(two_shape.shape, F32),
            pltpu.SemaphoreType.DMA((fours,)),
            pltpu.SemaphoreType.DMA((fours,)),
        ),
        into=pltpu.HBM,
        filled=True,
    )
    return output, grad_one, grad_two


def solution(mesh):
    rows = P(("region", "split"), None)
    columns = P(None, ("region", "split"))
    return jax.shard_map(
        shards,
        mesh=mesh,
        in_specs=(columns, P(), P(), rows, rows, columns),
        out_specs=(columns, P(), P()),
        check_vma=False,
    )
```
